32 devices in a mesh: feat: 8 (over z, core), dp: 4 (over y, x).
Axes of the slice: x: 2, y: 2, z: 4, core: 2. Of those that a mesh axis runs over, the one named last changes fastest.
Arguments:
- features: bfloat16 [4, 1024, 256], P('dp', 'feat'), may hold values from -6 to 6
- neigh_lists: int32 [4, 10, 128], P('dp'), may hold values from 0 to 255
- w1_self: bfloat16 [1024, 512], P('feat'), may hold values from -0.125 to 0.125
- w1_neigh: bfloat16 [1024, 512], P('feat'), may hold values from -0.125 to 0.125
- w2_self: bfloat16 [512, 512], replicated, may hold values from -0.1875 to 0.1875
- w2_neigh: bfloat16 [512, 512], replicated, may hold values from -0.1875 to 0.1875
- send_rows: int32 [4, 8, 4, 8], P('dp', 'feat'), may hold values from 0 to 15
- send_count: int32 [4, 8, 4], P('dp', 'feat'), may hold values from 1 to 8, as said below
- recv_target: int32 [4, 8, 4, 8], P('dp', 'feat'), may hold values from 0 to 15
- out_grad: bfloat16 [4, 8, 16, 512], P('dp', 'feat'), may hold values from -6 to 6
Outputs:
- layer_out: bfloat16 [4, 8, 16, 512], P('dp', 'feat')
- grad_w1_self: float32 [4, 1024, 512], P('dp', 'feat')
- grad_w1_neigh: float32 [4, 1024, 512], P('dp', 'feat')
The draws below stay inside these ranges and needn't reach their ends.
Inputs may be any that keep to these rules, and one draw needn't show every extreme that they name: `send_count`: for each feat index one data index, drawn from the seed, receives 8 live slots from every data peer; every other count is at most 4. `recv_target`: slots at or beyond the sending device's count carry nothing.
All inputs are finite; a program needn't handle non-finite values.
Results may differ from the reference program's by a relative error of at most 0.0277.
Values may be sent and summed in bfloat16 or wider, within the bound.
No kernel may reach another device: no remote copies, remote signals or barrier semaphores. Data moves between devices by JAX's collectives and lax.ppermute only.
A program may use at most 64 MiB of HBM per device.

```python
import jax
import jax.numpy as jnp
from jax import lax

D = 1024
H = 512
H2 = 512
ROW_DEV = 16
K1 = 10
CAP = 8
S = 128
SX = 256
N_FEAT = 8
N_DP = 4


def draw_send_count(key, part):
    key = jax.random.fold_in(key, 11)
    base_key, hot_key = jax.random.split(key)
    base = jax.random.randint(base_key, (N_DP, N_FEAT, N_DP), 1, CAP // 2 + 1)
    hottest = jax.random.randint(hot_key, (N_FEAT,), 0, N_DP)
    is_hot = jnp.arange(N_DP, dtype=jnp.int32)[None, :] == hottest[:, None]
    return jnp.where(is_hot[None, :, :], CAP, base).astype(jnp.int32)


def plant(values, own_key, low, largest):
    place = [jax.random.randint(jax.random.fold_in(own_key, axis), (), 0, length) for axis, length in enumerate(values.shape)]
    main_axis = values.shape.index(max(values.shape))
    next_to = place[:main_axis] + [(place[main_axis] + 1) % values.shape[main_axis]] + place[main_axis + 1:]
    return values.at[tuple(place)].set(low).at[tuple(next_to)].set(largest)


def level_of(key, extent, shards, smallest, high):
    gain = 1.0
    for axis_at, blocks in shards:
        draws = jax.random.uniform(jax.random.fold_in(jax.random.fold_in(key, 6), axis_at), (blocks,), jnp.float32, smallest / len(shards), high / len(shards))
        gain = gain * jnp.repeat(jnp.exp(draws), extent[axis_at] // blocks).reshape((-1,) + (1,) * (len(extent) - 1 - axis_at))
    return gain


def noise(stream_key, dims, width, reach, shards=(), kind=jnp.bfloat16):
    factor_of = level_of(stream_key, dims, shards, -0.22, 0.18) if shards else 1.0
    array = jax.random.normal(stream_key, dims, jnp.float32) * width * factor_of
    return jnp.minimum(jnp.maximum(array, -reach), reach).astype(kind)


def setup_inputs(seed: int = 0) -> dict:
    keys = jax.random.split(jax.random.key(seed), 11)
    return {
        "features": noise(keys[0], (N_DP, D, SX), 1.0, 6.0, ((0, 4), (1, 8))),
        "neigh_lists": plant(jax.random.randint(keys[1], (N_DP, K1, S), 0, SX), jax.random.fold_in(keys[1], 1), 0, SX - 1).astype(jnp.int32),
        "w1_self": noise(keys[2], (D, H), (2 * D) ** -0.5, 0.125, ((0, 8),)),
        "w1_neigh": noise(keys[3], (D, H), (2 * D) ** -0.5, 0.125, ((0, 8),)),
        "w2_self": noise(keys[4], (H, H2), (2 * H) ** -0.5, 0.1875),
        "w2_neigh": noise(keys[5], (H, H2), (2 * H) ** -0.5, 0.1875),
        "send_rows": plant(jax.random.randint(keys[6], (N_DP, N_FEAT, N_DP, CAP), 0, ROW_DEV), jax.random.fold_in(keys[6], 1), 0, ROW_DEV - 1).astype(jnp.int32),
        "send_count": draw_send_count(jax.random.fold_in(keys[10], 71), 0),
        "recv_target": plant(jax.random.randint(keys[8], (N_DP, N_FEAT, N_DP, CAP), 0, ROW_DEV), jax.random.fold_in(keys[8], 1), 0, ROW_DEV - 1).astype(jnp.int32),
        "out_grad": noise(keys[9], (N_DP, N_FEAT, ROW_DEV, H2), 1.0, 6.0, ((0, 4), (1, 8))),
    }


def first_layer(columns, neighbour_lists, w1_self, w1_neigh):
    self_cols = columns[:, :S]
    gathered = jnp.take(columns, neighbour_lists, axis=1)
    mean_cols = (jnp.sum(gathered.astype(jnp.float32), axis=1) / K1).astype(jnp.bfloat16)
    contract = (((0,), (0,)), ((), ()))
    preact = lax.dot_general(self_cols, w1_self, contract, preferred_element_type=jnp.float32)
    preact = preact + lax.dot_general(mean_cols, w1_neigh, contract, preferred_element_type=jnp.float32)
    return self_cols, mean_cols, preact


def add_rows(indices, values):
    zeroed = jnp.zeros((ROW_DEV, values.shape[-1]), jnp.float32)
    return zeroed.at[indices.reshape(-1)].add(values.reshape(-1, values.shape[-1]))


def reference(features, neigh_lists, w1_self, w1_neigh, w2_self, w2_neigh, send_rows, send_count, recv_target, out_grad):
    def group_step(inputs):
        return first_layer(inputs[0], inputs[1], w1_self, w1_neigh)

    self_all, mean_all, pre_all = lax.map(group_step, (features, neigh_lists))
    hidden = jnp.maximum(pre_all, 0.0).astype(jnp.bfloat16).reshape(N_DP, N_FEAT, ROW_DEV, H)
    transposed = (((1,), (1,)), ((), ()))

    def per_device(hidden_rows, contrib, targets, usable, upstream):
        neigh_sum = add_rows(targets, contrib)
        degree = jnp.zeros((ROW_DEV,), jnp.float32).at[targets.reshape(-1)].add(usable.reshape(-1).astype(jnp.float32))[:, None]
        mean_two = ((hidden_rows.astype(jnp.float32) + neigh_sum) / (1.0 + degree)).astype(jnp.bfloat16)
        output = jnp.dot(hidden_rows, w2_self, preferred_element_type=jnp.float32)
        output = (output + jnp.dot(mean_two, w2_neigh, preferred_element_type=jnp.float32)).astype(jnp.bfloat16)
        grad_self = lax.dot_general(upstream, w2_self, transposed, preferred_element_type=jnp.float32)
        grad_mean = lax.dot_general(upstream, w2_neigh, transposed, preferred_element_type=jnp.float32) / (1.0 + degree)
        returning = jnp.where(usable[..., None], jnp.take(grad_mean, targets, axis=0), 0.0)
        return output, grad_self + grad_mean, returning

    def second_layer(inputs):
        rows_feat, sends, counts, targets, upstream = inputs
        outgoing = jax.vmap(jnp.take, in_axes=(0, 0, None))(rows_feat, sends, 0)
        incoming = jnp.swapaxes(outgoing, 0, 1)
        slot_ids = jnp.arange(CAP, dtype=jnp.int32)
        usable = slot_ids[None, None, :] < jnp.swapaxes(counts, 0, 1)[:, :, None]
        contrib = jnp.where(usable[..., None], incoming.astype(jnp.float32), 0.0)
        outputs, grad_local, returning = jax.vmap(per_device)(rows_feat, contrib, targets, usable, upstream)
        arrived = jnp.swapaxes(returning, 0, 1)
        back_sum = jax.vmap(add_rows)(sends, arrived)
        return outputs, grad_local + back_sum

    outputs, grad_hidden = lax.map(second_layer, (jnp.swapaxes(hidden, 0, 1), jnp.swapaxes(send_rows, 0, 1), jnp.swapaxes(send_count, 0, 1), jnp.swapaxes(recv_target, 0, 1), jnp.swapaxes(out_grad, 0, 1)))
    layer_out = jnp.swapaxes(outputs, 0, 1)
    grad_hidden = jnp.swapaxes(grad_hidden, 0, 1).reshape(N_DP, S, H)
    grad_pre = jnp.where(pre_all > 0, grad_hidden, 0.0).astype(jnp.bfloat16)

    def weight_grads(inputs):
        self_cols, mean_cols, grad_rows = inputs
        return (jnp.dot(self_cols, grad_rows, preferred_element_type=jnp.float32), jnp.dot(mean_cols, grad_rows, preferred_element_type=jnp.float32))

    grad_w1_self, grad_w1_neigh = lax.map(weight_grads, (self_all, mean_all, grad_pre))
    return layer_out, grad_w1_self, grad_w1_neigh
```

```python
import functools

import jax
import jax.numpy as jnp
from jax import lax
from jax.experimental import pallas as pl
from jax.experimental.pallas import tpu as pltpu
from jax.sharding import PartitionSpec as P

K1 = 10
HIDDEN_COST = 3 * 10**8
OWN_COST = 10**8
BACKWARD_COST = 10**10
INDEX_COST = 10**8
F32 = jnp.float32
BF16 = jnp.bfloat16
NT = (((1,), (1,)), ((), ()))
TN = (((0,), (0,)), ((), ()))
VMEM = pl.BlockSpec(memory_space=pltpu.VMEM)
PARAMS = pltpu.CompilerParams(vmem_limit_bytes=12 * 1024 * 1024)


def iota(shape, dim):
    return lax.broadcasted_iota(jnp.int32, shape, dim)


def table_lanes(peers, slots):
    return -(-3 * peers * slots // 128) * 128


def first_layer_kernel(
    feat_hbm, lists_hbm, w1s_hbm, w1n_hbm, rows_hbm, counts_hbm, targets_hbm, og_hbm, w2s_hbm, w2n_hbm,
    keep_ref, send_ref, mean_ref, aux_ref, w2s_ref, w2n_ref,
    feat_ref, lists_ref, w1_ref, rows_ref, counts_ref, targets_ref, og_ref, both_ref, part_ref, sems,
):
    i = pl.program_id(0)
    depth = feat_ref.shape[1]
    pairs = (
        (lists_hbm, lists_ref), (feat_hbm, feat_ref),
        (w1s_hbm, w1_ref.at[0:depth]), (w1n_hbm, w1_ref.at[depth : 2 * depth]),
        (targets_hbm, targets_ref), (rows_hbm, rows_ref), (counts_hbm, counts_ref), (og_hbm, og_ref),
        (w2s_hbm, w2s_ref), (w2n_hbm, w2n_ref),
    )
    copies = [pltpu.make_async_copy(src, dst, sems.at[n]) for n, (src, dst) in enumerate(pairs)]

    def wait(first, last):
        @pl.when(i == 0)
        def _():
            for copy in copies[first:last]:
                copy.wait()

    @pl.when(i == 0)
    def _():
        for copy in copies:
            copy.start()

    core = lax.axis_index("feat") % 2
    nodes = feat_ref.shape[2]
    tile, width = part_ref.shape
    rows_dev = og_ref.shape[2]
    step = min(nodes, 256)
    at_tile = pl.ds(pl.multiple_of(i * tile, tile), tile)
    wait(0, 1)
    hits = []
    for start in range(0, nodes, step):
        ids = iota((step, tile), 0) + start
        times = jnp.zeros((step, tile), F32)
        for k in range(K1):
            times = times + (ids == lists_ref[k, :, at_tile]).astype(F32)
        hits.append(times.astype(BF16))
    wait(1, 2)
    total = jnp.zeros((depth, tile), F32)
    for n, times in enumerate(hits):
        total = total + jnp.dot(
            feat_ref[0, :, n * step : (n + 1) * step], times, preferred_element_type=F32
        )
    mean = (total / K1).astype(BF16)
    mean_ref[...] = mean
    both_ref[0:depth, :] = feat_ref[0, :, at_tile]
    both_ref[depth:, :] = mean
    wait(2, 4)
    part_ref[...] = lax.dot_general(both_ref[...], w1_ref[...], TN, preferred_element_type=F32)
    for z in range(keep_ref.shape[0]):
        for ref, which in ((keep_ref, core), (send_ref, 1 - core)):
            at = pl.multiple_of((2 * z + which) * rows_dev, rows_dev)
            ref[z] = part_ref[pl.ds(at, rows_dev), :]

    @pl.when(i == 0)
    def _():
        for copy in copies[4:]:
            copy.wait()
        peers, slots = rows_ref.shape[2], rows_ref.shape[3]
        lanes = aux_ref.shape[1] - width
        which = iota((slots, lanes), 1) // (peers * slots)
        same_slot = iota((slots, lanes), 1) % slots == iota((slots, lanes), 0)

        def tiled(ref, n):
            spread = (same_slot & (which == n)).astype(BF16)
            return jnp.dot(ref[0, 0].astype(BF16), spread, preferred_element_type=F32)

        eye = iota((peers, peers), 0) == iota((peers, peers), 1)
        column = jnp.sum(jnp.where(eye, counts_ref[0], 0), axis=1, keepdims=True)
        lane = iota((peers, lanes), 1)
        live = (lane // (peers * slots) == 2) & (lane % slots < column)
        tables = tiled(targets_ref, 0) + tiled(rows_ref, 1) + live.astype(F32)
        if peers < rows_dev:
            tables = jnp.concatenate([tables, jnp.zeros((rows_dev - peers, lanes), F32)], axis=0)
        aux_ref[:, :width] = og_ref[0, 0]
        aux_ref[:, width:] = tables.astype(BF16)


def first_layer(features, lists, w1s, w1n, rows, counts, targets, og, w2s, w2n):
    depth = features.shape[1]
    group, width = lists.shape[2], w1s.shape[1]
    lists = lists.reshape(lists.shape[1], 1, group)
    rows_dev = og.shape[2]
    tile = min(group, 128)
    chips = group // (2 * rows_dev)
    tile_chips = tile // (2 * rows_dev)
    aux = (rows_dev, width + table_lanes(*rows.shape[2:]))
    args = (features, lists, w1s, w1n, rows, counts, targets, og, w2s, w2n)
    args = tuple(pltpu.with_memory_space_constraint(a, pltpu.HBM) for a in args)
    half = jax.ShapeDtypeStruct((chips, rows_dev, width), F32)
    half_spec = pl.BlockSpec((tile_chips, rows_dev, width), lambda i: (i, 0, 0))
    whole = lambda shape: pl.BlockSpec(shape, lambda i: (0,) * len(shape))
    scratch = [features, lists, jax.ShapeDtypeStruct((2 * depth, width), BF16), rows, counts, targets, og]
    return pl.pallas_call(
        first_layer_kernel,
        grid=(group // tile,),
        in_specs=[pl.BlockSpec(memory_space=pltpu.HBM)] * len(args),
        out_specs=[
            half_spec, half_spec,
            pl.BlockSpec((depth, tile), lambda i: (0, i)),
            whole(aux), whole(w2s.shape), whole(w2n.shape),
        ],
        out_shape=[
            half, half,
            jax.ShapeDtypeStruct((depth, group), BF16),
            jax.ShapeDtypeStruct(aux, BF16),
            jax.ShapeDtypeStruct(w2s.shape, BF16),
            jax.ShapeDtypeStruct(w2n.shape, BF16),
        ],
        scratch_shapes=[pltpu.VMEM(a.shape, a.dtype) for a in scratch]
        + [pltpu.VMEM((2 * depth, tile), BF16), pltpu.VMEM((tile, width), F32)]
        + [pltpu.SemaphoreType.DMA((len(args),))],
        name="first_layer", compiler_params=PARAMS,
    )(*args)


def call(kernel, name, args, out_shape, cost=0):
    return pl.pallas_call(
        kernel,
        in_specs=[VMEM] * len(args),
        out_specs=[VMEM] * len(out_shape),
        out_shape=[jax.ShapeDtypeStruct(shape, dtype) for shape, dtype in out_shape],
        name=name, compiler_params=PARAMS,
        cost_estimate=pl.CostEstimate(flops=cost, bytes_accessed=0, transcendentals=0),
    )(*args)


def pair_sum_kernel(keep_ref, got_ref, near_ref, far_ref):
    z = lax.axis_index("feat") // 2
    for s in range(keep_ref.shape[0]):
        at = lax.bitwise_xor(z, s)
        (far_ref if s % 2 else near_ref)[s // 2] = keep_ref[at] + got_ref[at]


def pair_sum(keep, got):
    half = ((keep.shape[0] // 2,) + keep.shape[1:], F32)
    return call(pair_sum_kernel, "pair_sum", (keep, got), [half, half])


def fold_kernel(near_ref, got_ref, *outs):
    for s in range(near_ref.shape[0]):
        outs[s % len(outs)][s // len(outs)] = near_ref[s] + got_ref[s]


def fold(near, got, parts):
    out = ((near.shape[0] // parts,) + near.shape[1:], F32)
    return call(fold_kernel, "fold", (near, got), [out] * parts)


def join_kernel(a_ref, b_ref, out_ref):
    count = out_ref.shape[0] // 2
    out_ref[:count] = a_ref[:count]
    out_ref[count:] = b_ref[:count]


def join(a, b, cost=0):
    count = a.shape[0]
    return call(join_kernel, "join", (a, b), [((2 * count,) + a.shape[1:], a.dtype)], cost)[0]


def place(scratch, near, far, size, me):
    count = near.shape[0] // size
    for s in range(2 * count):
        ref, at = (near, s) if s < count else (far, s - count)
        to = pl.multiple_of(lax.bitwise_xor(me, s) * size, size)
        scratch[pl.ds(to, size), :] = ref[at * size : (at + 1) * size, :]


def near_kernel(near_ref, w2s_ref, w2n_ref, self_ref, near_grad_ref):
    rows, width = self_ref.shape
    self_ref[...] = lax.dot_general(near_ref[:rows, :width], w2s_ref[...], NT, preferred_element_type=F32)
    near_grad_ref[...] = lax.dot_general(near_ref[:, :width], w2n_ref[...], NT, preferred_element_type=F32)


def backward_near(near, w2s, w2n, rows_dev):
    width = w2s.shape[0]
    shapes = [((rows_dev, width), F32), ((near.shape[0], width), F32)]
    return call(near_kernel, "backward_near", (near, w2s, w2n), shapes)


def backward_kernel(
    peers, slots, near_ref, far_ref, self_ref, near_grad_ref, w2n_ref, grad_ref, table_ref, degree_ref,
    tables, grads,
):
    me = lax.axis_index("dp")
    rows, width = self_ref.shape
    place(tables, near_ref.at[:, width:], far_ref.at[:, width:], rows, me)
    far_grad = lax.dot_general(far_ref[:, :width], w2n_ref[...], NT, preferred_element_type=F32)
    place(grads, near_grad_ref, far_grad, rows, me)
    lanes = peers * slots

    def table(d, which):
        return tables[d * rows : (d + 1) * rows, which * lanes : (which + 1) * lanes].astype(F32)

    block_of = iota((rows, lanes), 1) // slots
    diagonal = iota((rows, lanes), 0) == block_of
    mine = iota((rows, lanes), 0) == me

    def pick(where, x):
        return jnp.sum(jnp.where(where, x, 0.0), axis=0, keepdims=True)

    def crossed(which):
        return sum(jnp.where(block_of == d, table(d, which), 0.0) for d in range(peers))

    def own(which):
        return sum(jnp.where(me == d, table(d, which), 0.0) for d in range(peers))

    live_in = crossed(2)
    target_there = pick(mine, crossed(0))
    row_there = pick(mine, crossed(1))
    own_target, own_row, own_live = [pick(diagonal, own(which)) for which in range(3)]
    own_live_in = pick(mine, live_in)

    local = iota((rows, lanes), 0).astype(F32)
    every = iota((peers * rows, lanes), 0)
    same = every // rows == iota((peers * rows, lanes), 1) // slots
    every_local = (every % rows).astype(F32)

    back = jnp.where(local == own_row, own_live, 0.0).astype(BF16)
    there = jnp.where(same & (every_local == target_there), 1.0, 0.0).astype(BF16)
    back_table = lax.dot_general(back, there, NT, preferred_element_type=F32)
    into = jnp.where(local == own_target, own_live_in, 0.0)
    origin = jnp.where(same & (every_local == row_there), 1.0, 0.0).astype(BF16)
    table_ref[...] = lax.dot_general(into.astype(BF16), origin, NT, preferred_element_type=F32).astype(BF16)
    degree_ref[...] = jnp.broadcast_to(jnp.sum(into, axis=1, keepdims=True), degree_ref.shape)

    own_columns = iota(back_table.shape, 1) - me * rows
    back_table = back_table + (own_columns == iota(back_table.shape, 0)).astype(F32)
    degrees = []
    for e in range(peers):
        hit = jnp.where(local == pick(diagonal, table(e, 0)), live_in[e : e + 1, :], 0.0)
        degrees.append(jnp.sum(hit, axis=1, keepdims=True))
    grad_mean = grads[...] / (1.0 + jnp.concatenate(degrees, axis=0))
    high = grad_mean.astype(BF16)
    low = (grad_mean - high.astype(F32)).astype(BF16)
    back_table = back_table.astype(BF16)
    grad_hidden = self_ref[...] + jnp.dot(back_table, high, preferred_element_type=F32)
    grad_hidden = grad_hidden + jnp.dot(back_table, low, preferred_element_type=F32)
    grad_ref[...] = grad_hidden.astype(BF16)


def backward(near, far, w2s, w2n, peers, slots, rows_dev):
    width = w2s.shape[0]
    grad_self, near_grad = backward_near(near, w2s, w2n, rows_dev)
    return pl.pallas_call(
        functools.partial(backward_kernel, peers, slots),
        in_specs=[VMEM] * 5,
        out_specs=[VMEM] * 3,
        out_shape=[
            jax.ShapeDtypeStruct((rows_dev, width), BF16),
            jax.ShapeDtypeStruct((rows_dev, peers * rows_dev), BF16),
            jax.ShapeDtypeStruct((rows_dev, 128), F32),
        ],
        scratch_shapes=[
            pltpu.VMEM((peers * rows_dev, near.shape[1] - width), BF16),
            pltpu.VMEM((peers * rows_dev, width), F32),
        ],
        name="second_backward", compiler_params=PARAMS,
        cost_estimate=pl.CostEstimate(flops=BACKWARD_COST, bytes_accessed=0, transcendentals=0),
    )(near, far, grad_self, near_grad, w2n)


def hidden_kernel(total_ref, got_ref, grad_ref, grad_far_ref, hidden_ref, grads_ref):
    for s, ref in enumerate((grad_ref, grad_far_ref)):
        preact = total_ref[s] + got_ref[1 - s]
        grads_ref[s] = jnp.where(preact > 0, ref[...], jnp.zeros_like(ref))
        if s == 0:
            hidden_ref[...] = jnp.maximum(preact, 0.0).astype(BF16)


def hidden_and_grads(total, got, grad, grad_far):
    return call(
        hidden_kernel, "hidden", (total, got, grad, grad_far), [(grad.shape, BF16), (total.shape, BF16)]
    )


def own_part_kernel(hidden_ref, w2s_ref, out_ref):
    out_ref[...] = jnp.dot(hidden_ref[...], w2s_ref[...], preferred_element_type=F32)


def own_part(hidden, w2s):
    out = ((hidden.shape[0], w2s.shape[1]), F32)
    return call(own_part_kernel, "own_part", (hidden, w2s), [out], OWN_COST)[0]


def outputs_kernel(codes, near_ref, far_ref, table_ref, degree_ref, own_ref, w2n_ref, *refs):
    grad_refs, (feat_ref, mean_ref, out_hbm, self_hbm, neigh_hbm) = refs[:-11], refs[-11:-6]
    out_ref, self_ref, neigh_ref, grad_scratch, hidden_scratch, sems = refs[-6:]
    pairs = ((self_ref, self_hbm), (neigh_ref, neigh_hbm), (out_ref, out_hbm))
    copies = [pltpu.make_async_copy(src, dst, sems.at[n]) for n, (src, dst) in enumerate(pairs)]
    rows = table_ref.shape[0]
    group = mean_ref.shape[1]
    me = lax.axis_index("feat")
    for ref, code_list in zip(grad_refs, codes):
        for n, code in enumerate(code_list):
            to = pl.multiple_of(lax.bitwise_xor(me, code) * rows, rows)
            grad_scratch[pl.ds(to, rows), :] = ref[n]
    grad_pre = grad_scratch[...]
    self_ref[0] = jnp.dot(feat_ref[0, :, :group], grad_pre, preferred_element_type=F32)
    copies[0].start()
    neigh_ref[0] = jnp.dot(mean_ref[...], grad_pre, preferred_element_type=F32)
    copies[1].start()

    place(hidden_scratch, near_ref, far_ref, rows, lax.axis_index("dp"))
    neigh_sum = jnp.dot(table_ref[...], hidden_scratch[...], preferred_element_type=F32)
    mean_two = ((near_ref[0:rows, :].astype(F32) + neigh_sum) / (1.0 + degree_ref[:, 0:1])).astype(BF16)
    out = own_ref[...] + jnp.dot(mean_two, w2n_ref[...], preferred_element_type=F32)
    out_ref[0, 0] = out.astype(BF16)
    copies[2].start()
    for copy in copies:
        copy.wait()


def outputs(near, far, table, degree, own, w2n, grads, codes, features, mean):
    group, width = mean.shape[1], grads[0].shape[2]
    grad = jax.ShapeDtypeStruct((1, mean.shape[0], width), F32)
    out = jax.ShapeDtypeStruct((1, 1) + own.shape, BF16)
    return pl.pallas_call(
        functools.partial(outputs_kernel, codes),
        in_specs=[VMEM] * (len(grads) + 8),
        out_specs=[pl.BlockSpec(memory_space=pltpu.HBM)] * 3,
        out_shape=[out, grad, grad],
        scratch_shapes=[pltpu.VMEM(a.shape, a.dtype) for a in (out, grad, grad)]
        + [pltpu.VMEM((group, width), BF16), pltpu.VMEM((table.shape[1], near.shape[1]), BF16)]
        + [pltpu.SemaphoreType.DMA((3,))],
        name="outputs", compiler_params=PARAMS,
    )(near, far, table, degree, own, w2n, *grads, features, mean)


def swap(x, axis, bits):
    return lax.ppermute(x, axis, [(i, i ^ bits) for i in range(lax.axis_size(axis))])


def far_half(near, axis):
    bits = 2
    while 2 * bits < lax.axis_size(axis):
        near = join(near, swap(near, axis, bits))
        bits *= 2
    return near, swap(near, axis, bits)


def sum_over_chips(near, far, chips):
    bit = 1
    while 4 * bit < chips:
        near, far = fold(near, swap(far, "feat", 2 * bit), 2)
        bit *= 2
    total = fold(near, swap(far, "feat", 2 * bit), 1)[0]
    return total, swap(total, "feat", chips)


def on_device(features, neigh_lists, w1_self, w1_neigh, w2_self, w2_neigh, send_rows, send_count, recv_target, out_grad):
    chips, peers = lax.axis_size("feat") // 2, lax.axis_size("dp")
    rows_dev, slots = out_grad.shape[2], send_rows.shape[3]
    keep, send, mean, aux, w2_self, w2_neigh = first_layer(
        features, neigh_lists, w1_self, w1_neigh, send_rows, send_count, recv_target, out_grad, w2_self, w2_neigh
    )
    near, far = pair_sum(keep, swap(send, "feat", 1))
    total, got = sum_over_chips(near, far, chips)
    aux_near, aux_far = far_half(join(aux, swap(aux, "dp", 1), INDEX_COST), "dp")
    grad, table, degree = backward(aux_near, aux_far, w2_self, w2_neigh, peers, slots, rows_dev)
    hidden, grads = hidden_and_grads(total, got, grad, swap(grad, "feat", chips))
    codes, bit = [0, chips // 2], chips // 4
    while bit > 1:
        grads = join(grads, swap(grads, "feat", 2 * bit))
        codes, bit = codes + [code ^ bit for code in codes], bit // 2
    grads = [grads, swap(grads, "feat", 2)]
    grads = grads + [swap(x, "feat", 1) for x in grads]
    codes = [[2 * code ^ flip for code in codes] for flip in (0, 2, 1, 3)]
    near, far = far_half(join(hidden, swap(hidden, "dp", 1), cost=HIDDEN_COST), "dp")
    own = own_part(hidden, w2_self)
    return outputs(near, far, table, degree, own, w2_neigh, grads, codes, features, mean)


def solution(mesh):
    in_specs = (
        P("dp", "feat", None),
        P("dp", None, None),
        P("feat", None),
        P("feat", None),
        P(),
        P(),
        P("dp", "feat", None, None),
        P("dp", "feat", None),
        P("dp", "feat", None, None),
        P("dp", "feat", None, None),
    )
    out_specs = (P("dp", "feat", None, None), P("dp", "feat", None), P("dp", "feat", None))
    return jax.shard_map(
        on_device, mesh=mesh, in_specs=in_specs, out_specs=out_specs, check_vma=False
    )
```

```python
import functools

import jax
import jax.numpy as jnp
from jax import lax
from jax.experimental import pallas as pl
from jax.experimental.pallas import tpu as pltpu
from jax.sharding import PartitionSpec as P

K1 = 10
HIDDEN_COST = 3 * 10**8
PREACT_COST = 4 * 10**8
OWN_COST = 10**8
BACKWARD_COST = 0
INDEX_COST = 10**9
F32 = jnp.float32
BF16 = jnp.bfloat16
NT = (((1,), (1,)), ((), ()))
TN = (((0,), (0,)), ((), ()))
VMEM = pl.BlockSpec(memory_space=pltpu.VMEM)
PARAMS = pltpu.CompilerParams(vmem_limit_bytes=12 * 1024 * 1024)


def iota(shape, dim):
    return lax.broadcasted_iota(jnp.int32, shape, dim)


def table_lanes(peers, slots):
    return -(-3 * peers * slots // 128) * 128


def first_layer_kernel(
    tiles, feat_hbm, lists_hbm, w1s_hbm, w1n_hbm, rows_hbm, counts_hbm, targets_hbm, og_hbm,
    keep_ref, send_ref, both_ref, aux_ref,
    feat_ref, lists_ref, w1_ref, rows_ref, counts_ref, targets_ref, og_ref, part_ref, sems,
):
    i = pl.program_id(0) if tiles > 1 else 0
    depth = feat_ref.shape[1]
    pairs = (
        (lists_hbm, lists_ref), (feat_hbm, feat_ref),
        (w1s_hbm, w1_ref.at[0:depth]), (w1n_hbm, w1_ref.at[depth : 2 * depth]),
        (targets_hbm, targets_ref), (rows_hbm, rows_ref), (counts_hbm, counts_ref), (og_hbm, og_ref),
    )
    copies = [pltpu.make_async_copy(src, dst, sems.at[n]) for n, (src, dst) in enumerate(pairs)]

    def once(step):
        if tiles > 1:
            pl.when(i == 0)(step)
        else:
            step()

    def wait(first, last):
        @once
        def _():
            for copy in copies[first:last]:
                copy.wait()

    @once
    def _():
        for copy in copies:
            copy.start()

    me = lax.axis_index("feat")
    core = me % 2
    nodes = feat_ref.shape[2]
    tile, width = part_ref.shape
    rows_dev = og_ref.shape[2]
    step = min(nodes, 256)
    at_tile = pl.ds(pl.multiple_of(i * tile, tile), tile) if tiles > 1 else slice(0, tile)
    wait(0, 1)
    hits = []
    for start in range(0, nodes, step):
        ids = iota((step, tile), 0) + start
        times = jnp.zeros((step, tile), F32)
        for k in range(K1):
            times = times + (ids == lists_ref[k, :, at_tile]).astype(F32)
        hits.append(times.astype(BF16))

    @once
    def _():
        for copy in copies[4:8]:
            copy.wait()
        peers, slots = rows_ref.shape[2], rows_ref.shape[3]
        lanes = aux_ref.shape[1] - width
        which = iota((slots, lanes), 1) // (peers * slots)
        same_slot = iota((slots, lanes), 1) % slots == iota((slots, lanes), 0)

        def tiled(ref, n):
            spread = (same_slot & (which == n)).astype(BF16)
            return jnp.dot(ref[0, 0].astype(BF16), spread, preferred_element_type=F32)

        eye = iota((peers, peers), 0) == iota((peers, peers), 1)
        column = jnp.sum(jnp.where(eye, counts_ref[0], 0), axis=1, keepdims=True)
        lane = iota((peers, lanes), 1)
        live = (lane // (peers * slots) == 2) & (lane % slots < column)
        tables = tiled(targets_ref, 0) + tiled(rows_ref, 1) + live.astype(F32)
        if peers < rows_dev:
            tables = jnp.concatenate([tables, jnp.zeros((rows_dev - peers, lanes), F32)], axis=0)
        aux_ref[:, :width] = og_ref[0, 0]
        aux_ref[:, width:] = tables.astype(BF16)

    wait(1, 2)
    total = jnp.zeros((depth, tile), F32)
    for n, times in enumerate(hits):
        total = total + jnp.dot(
            feat_ref[0, :, n * step : (n + 1) * step], times, preferred_element_type=F32
        )
    both_ref[0:depth, :] = feat_ref[0, :, at_tile]
    both_ref[depth:, :] = (total / K1).astype(BF16)
    wait(2, 4)
    part_ref[...] = lax.dot_general(both_ref[...], w1_ref[...], TN, preferred_element_type=F32)
    for z in range(keep_ref.shape[0]):
        kept = jnp.where(i * keep_ref.shape[0] + z == me // 2, core, 1 - core)
        for ref, which in ((keep_ref, kept), (send_ref, 1 - kept)):
            at = pl.multiple_of((2 * z + which) * rows_dev, rows_dev)
            ref[z] = part_ref[pl.ds(at, rows_dev), :]


def first_layer(features, lists, w1s, w1n, rows, counts, targets, og):
    depth = features.shape[1]
    group, width = lists.shape[2], w1s.shape[1]
    lists = lists.reshape(lists.shape[1], 1, group)
    rows_dev = og.shape[2]
    tile = min(group, 128)
    chips = group // (2 * rows_dev)
    tile_chips = tile // (2 * rows_dev)
    aux = (rows_dev, width + table_lanes(*rows.shape[2:]))
    args = (features, lists, w1s, w1n, rows, counts, targets, og)
    args = tuple(pltpu.with_memory_space_constraint(a, pltpu.HBM) for a in args)
    half = jax.ShapeDtypeStruct((chips, rows_dev, width), F32)
    half_spec = pl.BlockSpec((tile_chips, rows_dev, width), lambda i: (i, 0, 0))
    whole = lambda shape: pl.BlockSpec(shape, lambda i: (0,) * len(shape))
    scratch = [features, lists, jax.ShapeDtypeStruct((2 * depth, width), BF16), rows, counts, targets, og]
    return pl.pallas_call(
        functools.partial(first_layer_kernel, group // tile),
        grid=(group // tile,),
        in_specs=[pl.BlockSpec(memory_space=pltpu.HBM)] * len(args),
        out_specs=[
            half_spec, half_spec,
            pl.BlockSpec((2 * depth, tile), lambda i: (0, i)),
            whole(aux),
        ],
        out_shape=[
            half, half,
            jax.ShapeDtypeStruct((2 * depth, group), BF16),
            jax.ShapeDtypeStruct(aux, BF16),
        ],
        scratch_shapes=[pltpu.VMEM(a.shape, a.dtype) for a in scratch]
        + [pltpu.VMEM((tile, width), F32)]
        + [pltpu.SemaphoreType.DMA((len(args),))],
        name="first_layer", compiler_params=PARAMS,
    )(*args)


def call(kernel, name, args, out_shape, cost=0):
    return pl.pallas_call(
        kernel,
        in_specs=[VMEM] * len(args),
        out_specs=[VMEM] * len(out_shape),
        out_shape=[jax.ShapeDtypeStruct(shape, dtype) for shape, dtype in out_shape],
        name=name, compiler_params=PARAMS,
        cost_estimate=pl.CostEstimate(flops=cost, bytes_accessed=0, transcendentals=0),
    )(*args)


def reverse(n, levels):
    return sum(((n >> k) & 1) << (levels - 1 - k) for k in range(levels))


def code_of(n, levels, core):
    return jnp.where(core == 0, n, reverse(n, levels))


def levels_of(count):
    return count.bit_length() - 1


def pair_sum_kernel(keep_ref, got_ref, *outs):
    z = lax.axis_index("feat") // 2
    for s, ref in enumerate(outs):
        at = lax.bitwise_xor(z, s)
        ref[...] = keep_ref[at] + got_ref[at]


def pair_sum(keep, got):
    return call(pair_sum_kernel, "pair_sum", (keep, got), [(keep.shape[1:], F32)] * keep.shape[0])


def preact_kernel(*refs):
    refs[-1][...] = sum(ref[...] for ref in refs[:-1])


def preact_sum(parts):
    return call(preact_kernel, "preact", parts, [(parts[0].shape, F32)], PREACT_COST)[0]


def join_kernel(a_ref, b_ref, *refs):
    out_ref = refs[-1]
    count = a_ref.shape[0]
    out_ref[:count] = a_ref[...]
    out_ref[count:] = b_ref[...]


def join(a, b, cost=0, after=()):
    return call(join_kernel, "join", (a, b, *after), [((2 * a.shape[0],) + a.shape[1:], a.dtype)], cost)[0]


def place(scratch, near, far, size, me):
    count = near.shape[0] // size
    core = lax.axis_index("feat") % 2
    for s in range(2 * count):
        ref, at = (near, s) if s < count else (far, s - count)
        code = code_of(s, levels_of(2 * count), core)
        to = pl.multiple_of(lax.bitwise_xor(me, code) * size, size)
        scratch[pl.ds(to, size), :] = ref[at * size : (at + 1) * size, :]


def near_kernel(near_ref, w2s_hbm, w2n_hbm, self_ref, near_grad_ref, w2s_ref, w2n_ref, sems):
    pairs = ((w2s_hbm, w2s_ref), (w2n_hbm, w2n_ref))
    copies = [pltpu.make_async_copy(src, dst, sems.at[n]) for n, (src, dst) in enumerate(pairs)]
    for copy in copies:
        copy.start()
    rows, width = self_ref.shape
    copies[0].wait()
    self_ref[...] = lax.dot_general(near_ref[:rows, :width], w2s_ref[...], NT, preferred_element_type=F32)
    copies[1].wait()
    near_grad_ref[...] = lax.dot_general(near_ref[:, :width], w2n_ref[...], NT, preferred_element_type=F32)


def backward_near(near, w2s, w2n, rows_dev):
    width = w2s.shape[0]
    hbm = pl.BlockSpec(memory_space=pltpu.HBM)
    shapes = [((rows_dev, width), F32), ((near.shape[0], width), F32), (w2s.shape, BF16), (w2n.shape, BF16)]
    return pl.pallas_call(
        near_kernel,
        in_specs=[VMEM, hbm, hbm],
        out_specs=[VMEM] * 4,
        out_shape=[jax.ShapeDtypeStruct(shape, dtype) for shape, dtype in shapes],
        scratch_shapes=[pltpu.SemaphoreType.DMA((2,))],
        name="backward_near", compiler_params=PARAMS,
        cost_estimate=pl.CostEstimate(flops=0, bytes_accessed=0, transcendentals=0),
    )(near, *[pltpu.with_memory_space_constraint(w, pltpu.HBM) for w in (w2s, w2n)])


def backward_kernel(
    peers, slots, near_ref, far_ref, self_ref, near_grad_ref, w2n_ref, grad_ref, table_ref, degree_ref,
    tables, grads,
):
    me = lax.axis_index("dp")
    rows, width = self_ref.shape
    place(tables, near_ref.at[:, width:], far_ref.at[:, width:], rows, me)
    far_grad = lax.dot_general(far_ref[:, :width], w2n_ref[...], NT, preferred_element_type=F32)
    place(grads, near_grad_ref, far_grad, rows, me)
    lanes = peers * slots

    def table(d, which):
        return tables[d * rows : (d + 1) * rows, which * lanes : (which + 1) * lanes].astype(F32)

    block_of = iota((rows, lanes), 1) // slots
    diagonal = iota((rows, lanes), 0) == block_of
    mine = iota((rows, lanes), 0) == me

    def pick(where, x):
        return jnp.sum(jnp.where(where, x, 0.0), axis=0, keepdims=True)

    def crossed(which):
        return sum(jnp.where(block_of == d, table(d, which), 0.0) for d in range(peers))

    def own(which):
        return sum(jnp.where(me == d, table(d, which), 0.0) for d in range(peers))

    live_in = crossed(2)
    target_there = pick(mine, crossed(0))
    row_there = pick(mine, crossed(1))
    own_target, own_row, own_live = [pick(diagonal, own(which)) for which in range(3)]
    own_live_in = pick(mine, live_in)

    local = iota((rows, lanes), 0).astype(F32)
    every = iota((peers * rows, lanes), 0)
    same = every // rows == iota((peers * rows, lanes), 1) // slots
    every_local = (every % rows).astype(F32)

    back = jnp.where(local == own_row, own_live, 0.0).astype(BF16)
    there = jnp.where(same & (every_local == target_there), 1.0, 0.0).astype(BF16)
    back_table = lax.dot_general(back, there, NT, preferred_element_type=F32)
    into = jnp.where(local == own_target, own_live_in, 0.0)
    origin = jnp.where(same & (every_local == row_there), 1.0, 0.0).astype(BF16)
    table_ref[...] = lax.dot_general(into.astype(BF16), origin, NT, preferred_element_type=F32).astype(BF16)
    degree_ref[...] = jnp.broadcast_to(jnp.sum(into, axis=1, keepdims=True), degree_ref.shape)

    own_columns = iota(back_table.shape, 1) - me * rows
    back_table = back_table + (own_columns == iota(back_table.shape, 0)).astype(F32)
    degrees = []
    for e in range(peers):
        hit = jnp.where(local == pick(diagonal, table(e, 0)), live_in[e : e + 1, :], 0.0)
        degrees.append(jnp.sum(hit, axis=1, keepdims=True))
    grad_mean = grads[...] / (1.0 + jnp.concatenate(degrees, axis=0))
    high = grad_mean.astype(BF16)
    low = (grad_mean - high.astype(F32)).astype(BF16)
    back_table = back_table.astype(BF16)
    grad_hidden = self_ref[...] + jnp.dot(back_table, high, preferred_element_type=F32)
    grad_hidden = grad_hidden + jnp.dot(back_table, low, preferred_element_type=F32)
    grad_ref[...] = grad_hidden.astype(BF16)


def backward(near, far, w2s, w2n, peers, slots, rows_dev):
    width = w2s.shape[0]
    grad_self, near_grad, w2s, w2n = backward_near(near, w2s, w2n, rows_dev)
    grad, table, degree = pl.pallas_call(
        functools.partial(backward_kernel, peers, slots),
        in_specs=[VMEM] * 5,
        out_specs=[VMEM] * 3,
        out_shape=[
            jax.ShapeDtypeStruct((rows_dev, width), BF16),
            jax.ShapeDtypeStruct((rows_dev, peers * rows_dev), BF16),
            jax.ShapeDtypeStruct((rows_dev, 128), F32),
        ],
        scratch_shapes=[
            pltpu.VMEM((peers * rows_dev, near.shape[1] - width), BF16),
            pltpu.VMEM((peers * rows_dev, width), F32),
        ],
        name="second_backward", compiler_params=PARAMS,
        cost_estimate=pl.CostEstimate(flops=BACKWARD_COST, bytes_accessed=0, transcendentals=0),
    )(near, far, grad_self, near_grad, w2n)
    return grad, table, degree, w2s, w2n


def hidden_kernel(preact_ref, grad_ref, hidden_ref, grads_ref):
    preact = preact_ref[...]
    hidden_ref[...] = jnp.maximum(preact, 0.0).astype(BF16)
    grads_ref[0] = jnp.where(preact > 0, grad_ref[...], jnp.zeros_like(grad_ref))


def hidden_and_grads(preact, grad):
    return call(hidden_kernel, "hidden", (preact, grad), [(grad.shape, BF16), ((1,) + grad.shape, BF16)])


def own_part_kernel(hidden_ref, w2s_ref, out_ref):
    out_ref[...] = jnp.dot(hidden_ref[...], w2s_ref[...], preferred_element_type=F32)


def own_part(hidden, w2s):
    out = ((hidden.shape[0], w2s.shape[1]), F32)
    return call(own_part_kernel, "own_part", (hidden, w2s), [out], OWN_COST)[0]


def outputs_kernel(codes, near_ref, far_ref, table_ref, degree_ref, own_ref, w2n_ref, *refs):
    grad_refs, (both_ref, out_hbm, self_hbm, neigh_hbm) = refs[:-10], refs[-10:-6]
    out_ref, self_ref, neigh_ref, grad_scratch, hidden_scratch, sems = refs[-6:]
    depth = both_ref.shape[0] // 2
    half = depth // 2 if depth % 32 == 0 else depth
    pieces = [(ref, hbm, n, at) for n, (ref, hbm) in enumerate(((self_ref, self_hbm), (neigh_ref, neigh_hbm)))
              for at in range(0, depth, half)]
    pairs = [(ref.at[0, pl.ds(at, half)], hbm.at[0, pl.ds(at, half)]) for ref, hbm, _, at in pieces]
    pairs.append((out_ref, out_hbm))
    copies = [pltpu.make_async_copy(src, dst, sems.at[n]) for n, (src, dst) in enumerate(pairs)]
    rows = table_ref.shape[0]
    me = lax.axis_index("feat")
    for ref, code_list in zip(grad_refs, codes):
        for n, code in enumerate(code_list):
            to = pl.multiple_of(lax.bitwise_xor(me, code) * rows, rows)
            grad_scratch[pl.ds(to, rows), :] = ref[n]
    grad_pre = grad_scratch[...]
    for (ref, _, n, at), copy in zip(pieces, copies):
        columns = both_ref[n * depth + at : n * depth + at + half, :]
        ref[0, at : at + half] = jnp.dot(columns, grad_pre, preferred_element_type=F32)
        copy.start()

    width = hidden_scratch.shape[1]
    place(hidden_scratch, near_ref.at[:, :width], far_ref.at[:, :width], rows, lax.axis_index("dp"))
    neigh_sum = jnp.dot(table_ref[...], hidden_scratch[...], preferred_element_type=F32)
    mean_two = ((near_ref[0:rows, :width].astype(F32) + neigh_sum) / (1.0 + degree_ref[:, 0:1])).astype(BF16)
    out = own_ref[...] + jnp.dot(mean_two, w2n_ref[...], preferred_element_type=F32)
    out_ref[0, 0] = out.astype(BF16)
    copies[-1].start()
    for copy in copies:
        copy.wait()


def outputs(near, far, table, degree, own, w2n, grads, codes, both):
    group, width = both.shape[1], grads[0].shape[2]
    grad = jax.ShapeDtypeStruct((1, both.shape[0] // 2, width), F32)
    out = jax.ShapeDtypeStruct((1, 1) + own.shape, BF16)
    return pl.pallas_call(
        functools.partial(outputs_kernel, codes),
        in_specs=[VMEM] * (len(grads) + 7),
        out_specs=[pl.BlockSpec(memory_space=pltpu.HBM)] * 3,
        out_shape=[out, grad, grad],
        scratch_shapes=[pltpu.VMEM(a.shape, a.dtype) for a in (out, grad, grad)]
        + [pltpu.VMEM((group, width), BF16), pltpu.VMEM((table.shape[1], w2n.shape[0]), BF16)]
        + [pltpu.SemaphoreType.DMA((5,))],
        name="outputs", compiler_params=PARAMS,
    )(near, far, table, degree, own, w2n, *grads, both)


def swap_cores(x):
    return lax.ppermute(x, "feat", [(i, i ^ 1) for i in range(lax.axis_size("feat"))])


def swap_chips(x, bits):
    return lax.ppermute(x, "feat", [(i, i ^ (2 * bits + 1)) for i in range(lax.axis_size("feat"))])


def swap_peers(x, level):
    feats, peers = lax.axis_size("feat"), lax.axis_size("dp")
    bits = 1 << level, 1 << (levels_of(peers) - 1 - level)
    pairs = [(f * peers + d, f * peers + (d ^ bits[f % 2])) for f in range(feats) for d in range(peers)]
    return lax.ppermute(x, ("feat", "dp"), pairs)


def gather_peers(x, cost, after):
    levels = levels_of(lax.axis_size("dp"))
    for level in range(levels - 1):
        x = join(x, swap_peers(x, level), cost, after)
    return x, swap_peers(x, levels - 1)


def on_device(features, neigh_lists, w1_self, w1_neigh, w2_self, w2_neigh, send_rows, send_count, recv_target, out_grad):
    chips, peers = lax.axis_size("feat") // 2, lax.axis_size("dp")
    rows_dev, slots = out_grad.shape[2], send_rows.shape[3]
    keep, send, both, aux = first_layer(
        features, neigh_lists, w1_self, w1_neigh, send_rows, send_count, recv_target, out_grad
    )
    parts = list(pair_sum(keep, swap_cores(send)))
    far = [swap_chips(parts[s], s) for s in range(chips - 1, 0, -1)]
    aux_near, aux_far = gather_peers(aux, INDEX_COST, parts[:1])
    grad, table, degree, w2_self, w2_neigh = backward(
        aux_near, aux_far, w2_self, w2_neigh, peers, slots, rows_dev
    )
    hidden, grads = hidden_and_grads(preact_sum(parts[:1] + far), grad)
    pieces, codes, bits = [grads], [[0]], chips // 2
    while bits:
        pieces.append(swap_chips(grads, bits))
        codes.append([code ^ (2 * bits + 1) for known in codes for code in known])
        bits //= 2
        if bits:
            grads = join(grads, pieces[-1])
    near, far = gather_peers(hidden, HIDDEN_COST, (grads,))
    pieces = pieces + [swap_cores(x) for x in pieces]
    codes = codes + [[code ^ 1 for code in known] for known in codes]
    own = own_part(hidden, w2_self)
    return outputs(near, far, table, degree, own, w2_neigh, pieces, codes, both)


def solution(mesh):
    in_specs = (
        P("dp", "feat", None),
        P("dp", None, None),
        P("feat", None),
        P("feat", None),
        P(),
        P(),
        P("dp", "feat", None, None),
        P("dp", "feat", None),
        P("dp", "feat", None, None),
        P("dp", "feat", None, None),
    )
    out_specs = (P("dp", "feat", None, None), P("dp", "feat", None), P("dp", "feat", None))
    return jax.shard_map(
        on_device, mesh=mesh, in_specs=in_specs, out_specs=out_specs, check_vma=False
    )
```

```python
import functools

import jax
import jax.numpy as jnp
from jax import lax
from jax.experimental import pallas as pl
from jax.experimental.pallas import tpu as pltpu
from jax.sharding import PartitionSpec as P

K1 = 10
HIDDEN_COST = 3 * 10**8
PREACT_COST = 4 * 10**8
OWN_COST = 10**8
BACKWARD_COST = 0
INDEX_COST = 10**9
F32 = jnp.float32
BF16 = jnp.bfloat16
NT = (((1,), (1,)), ((), ()))
TN = (((0,), (0,)), ((), ()))
VMEM = pl.BlockSpec(memory_space=pltpu.VMEM)
PARAMS = pltpu.CompilerParams(vmem_limit_bytes=12 * 1024 * 1024)


def iota(shape, dim):
    return lax.broadcasted_iota(jnp.int32, shape, dim)


def table_lanes(peers, slots):
    return -(-3 * peers * slots // 128) * 128


def first_layer_kernel(
    tiles, feat_hbm, lists_hbm, w1s_hbm, w1n_hbm, rows_hbm, counts_hbm, targets_hbm, og_hbm,
    keep_ref, send_ref, both_ref, aux_ref,
    feat_ref, lists_ref, w1_ref, rows_ref, counts_ref, targets_ref, og_ref, part_ref, sems,
):
    i = pl.program_id(0) if tiles > 1 else 0
    depth = feat_ref.shape[1]
    pairs = (
        (lists_hbm, lists_ref), (feat_hbm, feat_ref),
        (w1s_hbm, w1_ref.at[0:depth]), (w1n_hbm, w1_ref.at[depth : 2 * depth]),
        (targets_hbm, targets_ref), (rows_hbm, rows_ref), (counts_hbm, counts_ref), (og_hbm, og_ref),
    )
    copies = [pltpu.make_async_copy(src, dst, sems.at[n]) for n, (src, dst) in enumerate(pairs)]

    def once(step):
        if tiles > 1:
            pl.when(i == 0)(step)
        else:
            step()

    def wait(first, last):
        @once
        def _():
            for copy in copies[first:last]:
                copy.wait()

    @once
    def _():
        for copy in copies:
            copy.start()

    me = lax.axis_index("feat")
    core = me % 2
    nodes = feat_ref.shape[2]
    tile, width = part_ref.shape
    rows_dev = og_ref.shape[2]
    step = min(nodes, 256)
    at_tile = pl.ds(pl.multiple_of(i * tile, tile), tile) if tiles > 1 else slice(0, tile)
    wait(0, 1)
    hits = []
    for start in range(0, nodes, step):
        ids = iota((step, tile), 0) + start
        times = jnp.zeros((step, tile), F32)
        for k in range(K1):
            times = times + (ids == lists_ref[k, :, at_tile]).astype(F32)
        hits.append(times.astype(BF16))

    @once
    def _():
        for copy in copies[4:8]:
            copy.wait()
        peers, slots = rows_ref.shape[2], rows_ref.shape[3]
        lanes = aux_ref.shape[1] - width
        which = iota((slots, lanes), 1) // (peers * slots)
        same_slot = iota((slots, lanes), 1) % slots == iota((slots, lanes), 0)

        def tiled(ref, n):
            spread = (same_slot & (which == n)).astype(BF16)
            return jnp.dot(ref[0, 0].astype(BF16), spread, preferred_element_type=F32)

        eye = iota((peers, peers), 0) == iota((peers, peers), 1)
        column = jnp.sum(jnp.where(eye, counts_ref[0], 0), axis=1, keepdims=True)
        lane = iota((peers, lanes), 1)
        live = (lane // (peers * slots) == 2) & (lane % slots < column)
        tables = tiled(targets_ref, 0) + tiled(rows_ref, 1) + live.astype(F32)
        if peers < rows_dev:
            tables = jnp.concatenate([tables, jnp.zeros((rows_dev - peers, lanes), F32)], axis=0)
        aux_ref[:, :width] = og_ref[0, 0]
        aux_ref[:, width:] = tables.astype(BF16)

    wait(1, 2)
    total = jnp.zeros((depth, tile), F32)
    for n, times in enumerate(hits):
        total = total + jnp.dot(
            feat_ref[0, :, n * step : (n + 1) * step], times, preferred_element_type=F32
        )
    both_ref[0:depth, :] = feat_ref[0, :, at_tile]
    both_ref[depth:, :] = (total / K1).astype(BF16)
    wait(2, 4)
    part_ref[...] = lax.dot_general(both_ref[...], w1_ref[...], TN, preferred_element_type=F32)
    for z in range(keep_ref.shape[0]):
        kept = jnp.where(i * keep_ref.shape[0] + z == me // 2, core, 1 - core)
        for ref, which in ((keep_ref, kept), (send_ref, 1 - kept)):
            at = pl.multiple_of((2 * z + which) * rows_dev, rows_dev)
            ref[z] = part_ref[pl.ds(at, rows_dev), :]


def first_layer(features, lists, w1s, w1n, rows, counts, targets, og):
    depth = features.shape[1]
    group, width = lists.shape[2], w1s.shape[1]
    lists = lists.reshape(lists.shape[1], 1, group)
    rows_dev = og.shape[2]
    tile = min(group, 128)
    chips = group // (2 * rows_dev)
    tile_chips = tile // (2 * rows_dev)
    aux = (rows_dev, width + table_lanes(*rows.shape[2:]))
    args = (features, lists, w1s, w1n, rows, counts, targets, og)
    args = tuple(pltpu.with_memory_space_constraint(a, pltpu.HBM) for a in args)
    half = jax.ShapeDtypeStruct((chips, rows_dev, width), F32)
    half_spec = pl.BlockSpec((tile_chips, rows_dev, width), lambda i: (i, 0, 0))
    whole = lambda shape: pl.BlockSpec(shape, lambda i: (0,) * len(shape))
    scratch = [features, lists, jax.ShapeDtypeStruct((2 * depth, width), BF16), rows, counts, targets, og]
    return pl.pallas_call(
        functools.partial(first_layer_kernel, group // tile),
        grid=(group // tile,),
        in_specs=[pl.BlockSpec(memory_space=pltpu.HBM)] * len(args),
        out_specs=[
            half_spec, half_spec,
            pl.BlockSpec((2 * depth, tile), lambda i: (0, i)),
            whole(aux),
        ],
        out_shape=[
            half, half,
            jax.ShapeDtypeStruct((2 * depth, group), BF16),
            jax.ShapeDtypeStruct(aux, BF16),
        ],
        scratch_shapes=[pltpu.VMEM(a.shape, a.dtype) for a in scratch]
        + [pltpu.VMEM((tile, width), F32)]
        + [pltpu.SemaphoreType.DMA((len(args),))],
        name="first_layer", compiler_params=PARAMS,
    )(*args)


def call(kernel, name, args, out_shape, cost=0):
    return pl.pallas_call(
        kernel,
        in_specs=[VMEM] * len(args),
        out_specs=[VMEM] * len(out_shape),
        out_shape=[jax.ShapeDtypeStruct(shape, dtype) for shape, dtype in out_shape],
        name=name, compiler_params=PARAMS,
        cost_estimate=pl.CostEstimate(flops=cost, bytes_accessed=0, transcendentals=0),
    )(*args)


def reverse(n, levels):
    return sum(((n >> k) & 1) << (levels - 1 - k) for k in range(levels))


def code_of(n, levels, core):
    return jnp.where(core == 0, n, reverse(n, levels))


def levels_of(count):
    return count.bit_length() - 1


def pair_sum_kernel(keep_ref, got_ref, *outs):
    z = lax.axis_index("feat") // 2
    for s, ref in enumerate(outs):
        at = lax.bitwise_xor(z, s)
        ref[...] = keep_ref[at] + got_ref[at]


def pair_sum(keep, got):
    return call(pair_sum_kernel, "pair_sum", (keep, got), [(keep.shape[1:], F32)] * keep.shape[0])


def preact_kernel(*refs):
    refs[-1][...] = sum(ref[...] for ref in refs[:-1])


def preact_sum(parts):
    return call(preact_kernel, "preact", parts, [(parts[0].shape, F32)], PREACT_COST)[0]


def join_kernel(a_ref, b_ref, *refs):
    out_ref = refs[-1]
    count = a_ref.shape[0]
    out_ref[:count] = a_ref[...]
    out_ref[count:] = b_ref[...]


def join(a, b, cost=0, after=()):
    return call(join_kernel, "join", (a, b, *after), [((2 * a.shape[0],) + a.shape[1:], a.dtype)], cost)[0]


def near_kernel(near_ref, w2s_hbm, w2n_hbm, self_ref, near_grad_ref, w2s_ref, w2n_ref, sems):
    pairs = ((w2s_hbm, w2s_ref), (w2n_hbm, w2n_ref))
    copies = [pltpu.make_async_copy(src, dst, sems.at[n]) for n, (src, dst) in enumerate(pairs)]
    for copy in copies:
        copy.start()
    rows, width = self_ref.shape
    copies[0].wait()
    self_ref[...] = lax.dot_general(near_ref[:rows, :width], w2s_ref[...], NT, preferred_element_type=F32)
    copies[1].wait()
    near_grad_ref[...] = lax.dot_general(near_ref[:, :width], w2n_ref[...], NT, preferred_element_type=F32)


def backward_near(near, w2s, w2n, rows_dev):
    width = w2s.shape[0]
    hbm = pl.BlockSpec(memory_space=pltpu.HBM)
    shapes = [((rows_dev, width), F32), ((near.shape[0], width), F32), (w2s.shape, BF16), (w2n.shape, BF16)]
    return pl.pallas_call(
        near_kernel,
        in_specs=[VMEM, hbm, hbm],
        out_specs=[VMEM] * 4,
        out_shape=[jax.ShapeDtypeStruct(shape, dtype) for shape, dtype in shapes],
        scratch_shapes=[pltpu.SemaphoreType.DMA((2,))],
        name="backward_near", compiler_params=PARAMS,
        cost_estimate=pl.CostEstimate(flops=0, bytes_accessed=0, transcendentals=0),
    )(near, *[pltpu.with_memory_space_constraint(w, pltpu.HBM) for w in (w2s, w2n)])


def backward_kernel(
    peers, slots, near_ref, far_ref, self_ref, near_grad_ref, w2n_ref, grad_ref, table_ref, degree_ref
):
    me, core = lax.axis_index("dp"), lax.axis_index("feat") % 2
    rows, width = self_ref.shape
    lanes = peers * slots
    far_grad = lax.dot_general(far_ref[:, :width], w2n_ref[...], NT, preferred_element_type=F32)
    grads = jnp.concatenate([near_grad_ref[...], far_grad], axis=0)
    peer = [lax.bitwise_xor(me, code_of(s, levels_of(peers), core)) for s in range(peers)]

    def table(s, which):
        ref, at = (near_ref, s) if s < peers // 2 else (far_ref, s - peers // 2)
        at_lanes = slice(width + which * lanes, width + (which + 1) * lanes)
        return ref[at * rows : (at + 1) * rows, at_lanes].astype(F32)

    block_of = iota((rows, lanes), 1) // slots
    row_of = iota((rows, lanes), 0)
    diagonal = row_of == block_of

    def pick(where, x):
        return jnp.sum(jnp.where(where, x, 0.0), axis=0, keepdims=True)

    def crossed(which):
        return sum(jnp.where(block_of == peer[s], table(s, which), 0.0) for s in range(peers))

    live_in = crossed(2)
    mine = row_of == me
    target_there = pick(mine, crossed(0))
    row_there = pick(mine, crossed(1))
    own_target, own_row, own_live = [pick(diagonal, table(0, which)) for which in range(3)]
    own_live_in = pick(mine, live_in)

    local = row_of.astype(F32)
    every = iota((peers * rows, lanes), 0)
    peer_of = sum(jnp.where(every // rows == s, peer[s], 0) for s in range(peers))
    same = peer_of == iota((peers * rows, lanes), 1) // slots
    every_local = (every % rows).astype(F32)

    back = jnp.where(local == own_row, own_live, 0.0).astype(BF16)
    there = jnp.where(same & (every_local == target_there), 1.0, 0.0).astype(BF16)
    back_table = lax.dot_general(back, there, NT, preferred_element_type=F32)
    into = jnp.where(local == own_target, own_live_in, 0.0)
    origin = jnp.where(same & (every_local == row_there), 1.0, 0.0).astype(BF16)
    table_ref[...] = lax.dot_general(into.astype(BF16), origin, NT, preferred_element_type=F32).astype(BF16)
    degree_ref[...] = jnp.broadcast_to(jnp.sum(into, axis=1, keepdims=True), degree_ref.shape)

    back_table = back_table + (iota(back_table.shape, 1) == iota(back_table.shape, 0)).astype(F32)
    degrees = []
    for s in range(peers):
        hit = jnp.where(local == pick(diagonal, table(s, 0)), pick(row_of == peer[s], live_in), 0.0)
        degrees.append(jnp.sum(hit, axis=1, keepdims=True))
    grad_mean = grads / (1.0 + jnp.concatenate(degrees, axis=0))
    high = grad_mean.astype(BF16)
    low = (grad_mean - high.astype(F32)).astype(BF16)
    back_table = back_table.astype(BF16)
    grad_hidden = self_ref[...] + jnp.dot(back_table, high, preferred_element_type=F32)
    grad_hidden = grad_hidden + jnp.dot(back_table, low, preferred_element_type=F32)
    grad_ref[...] = grad_hidden.astype(BF16)


def backward(near, far, w2s, w2n, peers, slots, rows_dev):
    width = w2s.shape[0]
    grad_self, near_grad, w2s, w2n = backward_near(near, w2s, w2n, rows_dev)
    grad, table, degree = pl.pallas_call(
        functools.partial(backward_kernel, peers, slots),
        in_specs=[VMEM] * 5,
        out_specs=[VMEM] * 3,
        out_shape=[
            jax.ShapeDtypeStruct((rows_dev, width), BF16),
            jax.ShapeDtypeStruct((rows_dev, peers * rows_dev), BF16),
            jax.ShapeDtypeStruct((rows_dev, 128), F32),
        ],
        name="second_backward", compiler_params=PARAMS,
        cost_estimate=pl.CostEstimate(flops=BACKWARD_COST, bytes_accessed=0, transcendentals=0),
    )(near, far, grad_self, near_grad, w2n)
    return grad, table, degree, w2s, w2n


def hidden_kernel(preact_ref, grad_ref, hidden_ref, grads_ref):
    preact = preact_ref[...]
    hidden_ref[...] = jnp.maximum(preact, 0.0).astype(BF16)
    grads_ref[0] = jnp.where(preact > 0, grad_ref[...], jnp.zeros_like(grad_ref))


def hidden_and_grads(preact, grad):
    return call(hidden_kernel, "hidden", (preact, grad), [(grad.shape, BF16), ((1,) + grad.shape, BF16)])


def own_part_kernel(hidden_ref, w2s_ref, out_ref):
    out_ref[...] = jnp.dot(hidden_ref[...], w2s_ref[...], preferred_element_type=F32)


def own_part(hidden, w2s):
    out = ((hidden.shape[0], w2s.shape[1]), F32)
    return call(own_part_kernel, "own_part", (hidden, w2s), [out], OWN_COST)[0]


def outputs_kernel(codes, near_ref, far_ref, table_ref, degree_ref, own_ref, w2n_ref, *refs):
    grad_refs, (both_ref, out_hbm, self_hbm, neigh_hbm) = refs[:-9], refs[-9:-5]
    out_ref, self_ref, neigh_ref, grad_scratch, sems = refs[-5:]
    depth = both_ref.shape[0] // 2
    half = depth // 2 if depth % 32 == 0 else depth
    pieces = [(ref, hbm, n, at) for n, (ref, hbm) in enumerate(((self_ref, self_hbm), (neigh_ref, neigh_hbm)))
              for at in range(0, depth, half)]
    pairs = [(ref.at[0, pl.ds(at, half)], hbm.at[0, pl.ds(at, half)]) for ref, hbm, _, at in pieces]
    pairs.append((out_ref, out_hbm))
    copies = [pltpu.make_async_copy(src, dst, sems.at[n]) for n, (src, dst) in enumerate(pairs)]
    rows = table_ref.shape[0]
    me = lax.axis_index("feat")
    for ref, code_list in zip(grad_refs, codes):
        for n, code in enumerate(code_list):
            to = pl.multiple_of(lax.bitwise_xor(me, code) * rows, rows)
            grad_scratch[pl.ds(to, rows), :] = ref[n]
    grad_pre = grad_scratch[...]
    for (ref, _, n, at), copy in zip(pieces, copies):
        columns = both_ref[n * depth + at : n * depth + at + half, :]
        ref[0, at : at + half] = jnp.dot(columns, grad_pre, preferred_element_type=F32)
        copy.start()

    count = near_ref.shape[0]
    neigh_sum = jnp.dot(table_ref[:, :count], near_ref[...], preferred_element_type=F32)
    neigh_sum = neigh_sum + jnp.dot(table_ref[:, count:], far_ref[...], preferred_element_type=F32)
    mean_two = ((near_ref[0:rows, :].astype(F32) + neigh_sum) / (1.0 + degree_ref[:, 0:1])).astype(BF16)
    out = own_ref[...] + jnp.dot(mean_two, w2n_ref[...], preferred_element_type=F32)
    out_ref[0, 0] = out.astype(BF16)
    copies[-1].start()
    for copy in copies:
        copy.wait()


def outputs(near, far, table, degree, own, w2n, grads, codes, both):
    group, width = both.shape[1], grads[0].shape[2]
    grad = jax.ShapeDtypeStruct((1, both.shape[0] // 2, width), F32)
    out = jax.ShapeDtypeStruct((1, 1) + own.shape, BF16)
    return pl.pallas_call(
        functools.partial(outputs_kernel, codes),
        in_specs=[VMEM] * (len(grads) + 7),
        out_specs=[pl.BlockSpec(memory_space=pltpu.HBM)] * 3,
        out_shape=[out, grad, grad],
        scratch_shapes=[pltpu.VMEM(a.shape, a.dtype) for a in (out, grad, grad)]
        + [pltpu.VMEM((group, width), BF16), pltpu.SemaphoreType.DMA((5,))],
        name="outputs", compiler_params=PARAMS,
    )(near, far, table, degree, own, w2n, *grads, both)


def swap_cores(x):
    return lax.ppermute(x, "feat", [(i, i ^ 1) for i in range(lax.axis_size("feat"))])


def swap_chips(x, bits):
    return lax.ppermute(x, "feat", [(i, i ^ (2 * bits + 1)) for i in range(lax.axis_size("feat"))])


def swap_peers(x, level):
    feats, peers = lax.axis_size("feat"), lax.axis_size("dp")
    bits = 1 << level, 1 << (levels_of(peers) - 1 - level)
    pairs = [(f * peers + d, f * peers + (d ^ bits[f % 2])) for f in range(feats) for d in range(peers)]
    return lax.ppermute(x, ("feat", "dp"), pairs)


def gather_peers(x, cost, after):
    levels = levels_of(lax.axis_size("dp"))
    for level in range(levels - 1):
        x = join(x, swap_peers(x, level), cost, after)
    return x, swap_peers(x, levels - 1)


def on_device(features, neigh_lists, w1_self, w1_neigh, w2_self, w2_neigh, send_rows, send_count, recv_target, out_grad):
    chips, peers = lax.axis_size("feat") // 2, lax.axis_size("dp")
    rows_dev, slots = out_grad.shape[2], send_rows.shape[3]
    keep, send, both, aux = first_layer(
        features, neigh_lists, w1_self, w1_neigh, send_rows, send_count, recv_target, out_grad
    )
    parts = list(pair_sum(keep, swap_cores(send)))
    order = [chips // 2] + [s for s in range(chips - 1, 0, -1) if s != chips // 2]
    far = [swap_chips(parts[s], s) for s in order]
    aux_near, aux_far = gather_peers(aux, INDEX_COST, parts[:1])
    grad, table, degree, w2_self, w2_neigh = backward(
        aux_near, aux_far, w2_self, w2_neigh, peers, slots, rows_dev
    )
    hidden, grads = hidden_and_grads(preact_sum(parts[:1] + far), grad)
    pieces, codes, bits = [grads], [[0]], chips // 2
    while bits:
        pieces.append(swap_chips(grads, bits))
        codes.append([code ^ (2 * bits + 1) for known in codes for code in known])
        bits //= 2
        if bits:
            grads = join(grads, pieces[-1])
    near, far = gather_peers(hidden, HIDDEN_COST, (grads,))
    pieces = pieces + [swap_cores(x) for x in pieces]
    codes = codes + [[code ^ 1 for code in known] for known in codes]
    own = own_part(hidden, w2_self)
    return outputs(near, far, table, degree, own, w2_neigh, pieces, codes, both)


def solution(mesh):
    in_specs = (
        P("dp", "feat", None),
        P("dp", None, None),
        P("feat", None),
        P("feat", None),
        P(),
        P(),
        P("dp", "feat", None, None),
        P("dp", "feat", None),
        P("dp", "feat", None, None),
        P("dp", "feat", None, None),
    )
    out_specs = (P("dp", "feat", None, None), P("dp", "feat", None), P("dp", "feat", None))
    return jax.shard_map(
        on_device, mesh=mesh, in_specs=in_specs, out_specs=out_specs, check_vma=False
    )
```

```python
import functools

import jax
import jax.numpy as jnp
from jax import lax
from jax.experimental import pallas as pl
from jax.experimental.pallas import tpu as pltpu
from jax.sharding import PartitionSpec as P

K1 = 10
HIDDEN_COST = 3 * 10**8
PREACT_COST = 4 * 10**8
OWN_COST = 10**8
MEAN_COST = 10**8
BACKWARD_COST = 0
INDEX_COST = 10**9
F32 = jnp.float32
BF16 = jnp.bfloat16
NT = (((1,), (1,)), ((), ()))
TN = (((0,), (0,)), ((), ()))
VMEM = pl.BlockSpec(memory_space=pltpu.VMEM)
PARAMS = pltpu.CompilerParams(vmem_limit_bytes=12 * 1024 * 1024)


def iota(shape, dim):
    return lax.broadcasted_iota(jnp.int32, shape, dim)


def table_lanes(peers, slots):
    return -(-3 * peers * slots // 128) * 128


def first_layer_kernel(
    tiles, feat_hbm, lists_hbm, w1s_hbm, w1n_hbm, rows_hbm, counts_hbm, targets_hbm, og_hbm,
    keep_ref, send_ref, both_ref, aux_ref,
    feat_ref, lists_ref, w1_ref, rows_ref, counts_ref, targets_ref, og_ref, part_ref, sems,
):
    i = pl.program_id(0) if tiles > 1 else 0
    depth = feat_ref.shape[1]
    pairs = (
        (lists_hbm, lists_ref), (feat_hbm, feat_ref),
        (w1s_hbm, w1_ref.at[0:depth]), (w1n_hbm, w1_ref.at[depth : 2 * depth]),
        (targets_hbm, targets_ref), (rows_hbm, rows_ref), (counts_hbm, counts_ref), (og_hbm, og_ref),
    )
    copies = [pltpu.make_async_copy(src, dst, sems.at[n]) for n, (src, dst) in enumerate(pairs)]

    def once(step):
        if tiles > 1:
            pl.when(i == 0)(step)
        else:
            step()

    def wait(first, last):
        @once
        def _():
            for copy in copies[first:last]:
                copy.wait()

    @once
    def _():
        for copy in copies:
            copy.start()

    me = lax.axis_index("feat")
    core = me % 2
    nodes = feat_ref.shape[2]
    tile, width = part_ref.shape
    rows_dev = og_ref.shape[2]
    step = min(nodes, 256)
    at_tile = pl.ds(pl.multiple_of(i * tile, tile), tile) if tiles > 1 else slice(0, tile)
    wait(0, 1)
    hits = []
    for start in range(0, nodes, step):
        ids = iota((step, tile), 0) + start
        times = jnp.zeros((step, tile), F32)
        for k in range(K1):
            times = times + (ids == lists_ref[k, :, at_tile]).astype(F32)
        hits.append(times.astype(BF16))

    @once
    def _():
        for copy in copies[4:8]:
            copy.wait()
        peers, slots = rows_ref.shape[2], rows_ref.shape[3]
        lanes = aux_ref.shape[1] - width
        which = iota((slots, lanes), 1) // (peers * slots)
        same_slot = iota((slots, lanes), 1) % slots == iota((slots, lanes), 0)

        def tiled(ref, n):
            spread = (same_slot & (which == n)).astype(BF16)
            return jnp.dot(ref[0, 0].astype(BF16), spread, preferred_element_type=F32)

        eye = iota((peers, peers), 0) == iota((peers, peers), 1)
        column = jnp.sum(jnp.where(eye, counts_ref[0], 0), axis=1, keepdims=True)
        lane = iota((peers, lanes), 1)
        live = (lane // (peers * slots) == 2) & (lane % slots < column)
        tables = tiled(targets_ref, 0) + tiled(rows_ref, 1) + live.astype(F32)
        if peers < rows_dev:
            tables = jnp.concatenate([tables, jnp.zeros((rows_dev - peers, lanes), F32)], axis=0)
        aux_ref[:, :width] = og_ref[0, 0]
        aux_ref[:, width:] = tables.astype(BF16)

    wait(1, 2)
    total = jnp.zeros((depth, tile), F32)
    for n, times in enumerate(hits):
        total = total + jnp.dot(
            feat_ref[0, :, n * step : (n + 1) * step], times, preferred_element_type=F32
        )
    both_ref[0:depth, :] = feat_ref[0, :, at_tile]
    both_ref[depth:, :] = (total / K1).astype(BF16)
    wait(2, 4)
    part_ref[...] = lax.dot_general(both_ref[...], w1_ref[...], TN, preferred_element_type=F32)
    for z in range(keep_ref.shape[0]):
        kept = jnp.where(i * keep_ref.shape[0] + z == me // 2, core, 1 - core)
        for ref, which in ((keep_ref, kept), (send_ref, 1 - kept)):
            at = pl.multiple_of((2 * z + which) * rows_dev, rows_dev)
            ref[z] = part_ref[pl.ds(at, rows_dev), :]


def first_layer(features, lists, w1s, w1n, rows, counts, targets, og):
    depth = features.shape[1]
    group, width = lists.shape[2], w1s.shape[1]
    lists = lists.reshape(lists.shape[1], 1, group)
    rows_dev = og.shape[2]
    tile = min(group, 128)
    chips = group // (2 * rows_dev)
    tile_chips = tile // (2 * rows_dev)
    aux = (rows_dev, width + table_lanes(*rows.shape[2:]))
    args = (features, lists, w1s, w1n, rows, counts, targets, og)
    args = tuple(pltpu.with_memory_space_constraint(a, pltpu.HBM) for a in args)
    half = jax.ShapeDtypeStruct((chips, rows_dev, width), F32)
    half_spec = pl.BlockSpec((tile_chips, rows_dev, width), lambda i: (i, 0, 0))
    whole = lambda shape: pl.BlockSpec(shape, lambda i: (0,) * len(shape))
    scratch = [features, lists, jax.ShapeDtypeStruct((2 * depth, width), BF16), rows, counts, targets, og]
    return pl.pallas_call(
        functools.partial(first_layer_kernel, group // tile),
        grid=(group // tile,),
        in_specs=[pl.BlockSpec(memory_space=pltpu.HBM)] * len(args),
        out_specs=[
            half_spec, half_spec,
            pl.BlockSpec((2 * depth, tile), lambda i: (0, i)),
            whole(aux),
        ],
        out_shape=[
            half, half,
            jax.ShapeDtypeStruct((2 * depth, group), BF16),
            jax.ShapeDtypeStruct(aux, BF16),
        ],
        scratch_shapes=[pltpu.VMEM(a.shape, a.dtype) for a in scratch]
        + [pltpu.VMEM((tile, width), F32)]
        + [pltpu.SemaphoreType.DMA((len(args),))],
        name="first_layer", compiler_params=PARAMS,
    )(*args)


def call(kernel, name, args, out_shape, cost=0):
    return pl.pallas_call(
        kernel,
        in_specs=[VMEM] * len(args),
        out_specs=[VMEM] * len(out_shape),
        out_shape=[jax.ShapeDtypeStruct(shape, dtype) for shape, dtype in out_shape],
        name=name, compiler_params=PARAMS,
        cost_estimate=pl.CostEstimate(flops=cost, bytes_accessed=0, transcendentals=0),
    )(*args)


def reverse(n, levels):
    return sum(((n >> k) & 1) << (levels - 1 - k) for k in range(levels))


def code_of(n, levels, core):
    return jnp.where(core == 0, n, reverse(n, levels))


def levels_of(count):
    return count.bit_length() - 1


def pair_sum_kernel(keep_ref, got_ref, *outs):
    z = lax.axis_index("feat") // 2
    for s, ref in enumerate(outs):
        at = lax.bitwise_xor(z, s)
        ref[...] = keep_ref[at] + got_ref[at]


def pair_sum(keep, got):
    return call(pair_sum_kernel, "pair_sum", (keep, got), [(keep.shape[1:], F32)] * keep.shape[0])


def preact_kernel(*refs):
    refs[-1][...] = sum(ref[...] for ref in refs[:-1])


def preact_sum(parts):
    return call(preact_kernel, "preact", parts, [(parts[0].shape, F32)], PREACT_COST)[0]


def join_kernel(a_ref, b_ref, *refs):
    out_ref = refs[-1]
    count = a_ref.shape[0]
    out_ref[:count] = a_ref[...]
    out_ref[count:] = b_ref[...]


def join(a, b, cost=0, after=()):
    return call(join_kernel, "join", (a, b, *after), [((2 * a.shape[0],) + a.shape[1:], a.dtype)], cost)[0]


def near_kernel(near_ref, w2s_hbm, w2n_hbm, self_ref, near_grad_ref, w2s_ref, w2n_ref, sems):
    pairs = ((w2s_hbm, w2s_ref), (w2n_hbm, w2n_ref))
    copies = [pltpu.make_async_copy(src, dst, sems.at[n]) for n, (src, dst) in enumerate(pairs)]
    for copy in copies:
        copy.start()
    rows, width = self_ref.shape
    copies[0].wait()
    self_ref[...] = lax.dot_general(near_ref[:rows, :width], w2s_ref[...], NT, preferred_element_type=F32)
    copies[1].wait()
    near_grad_ref[...] = lax.dot_general(near_ref[:, :width], w2n_ref[...], NT, preferred_element_type=F32)


def backward_near(near, w2s, w2n, rows_dev):
    width = w2s.shape[0]
    hbm = pl.BlockSpec(memory_space=pltpu.HBM)
    shapes = [((rows_dev, width), F32), ((near.shape[0], width), F32), (w2s.shape, BF16), (w2n.shape, BF16)]
    return pl.pallas_call(
        near_kernel,
        in_specs=[VMEM, hbm, hbm],
        out_specs=[VMEM] * 4,
        out_shape=[jax.ShapeDtypeStruct(shape, dtype) for shape, dtype in shapes],
        scratch_shapes=[pltpu.SemaphoreType.DMA((2,))],
        name="backward_near", compiler_params=PARAMS,
        cost_estimate=pl.CostEstimate(flops=0, bytes_accessed=0, transcendentals=0),
    )(near, *[pltpu.with_memory_space_constraint(w, pltpu.HBM) for w in (w2s, w2n)])


def backward_kernel(
    peers, slots, near_ref, far_ref, self_ref, near_grad_ref, w2n_ref, grad_ref, table_ref, degree_ref
):
    me, core = lax.axis_index("dp"), lax.axis_index("feat") % 2
    rows, width = self_ref.shape
    lanes = peers * slots
    far_grad = lax.dot_general(far_ref[:, :width], w2n_ref[...], NT, preferred_element_type=F32)
    grads = jnp.concatenate([near_grad_ref[...], far_grad], axis=0)
    peer = [lax.bitwise_xor(me, code_of(s, levels_of(peers), core)) for s in range(peers)]

    def table(s, which):
        ref, at = (near_ref, s) if s < peers // 2 else (far_ref, s - peers // 2)
        at_lanes = slice(width + which * lanes, width + (which + 1) * lanes)
        return ref[at * rows : (at + 1) * rows, at_lanes].astype(F32)

    block_of = iota((rows, lanes), 1) // slots
    row_of = iota((rows, lanes), 0)
    diagonal = row_of == block_of

    def pick(where, x):
        return jnp.sum(jnp.where(where, x, 0.0), axis=0, keepdims=True)

    def crossed(which):
        return sum(jnp.where(block_of == peer[s], table(s, which), 0.0) for s in range(peers))

    live_in = crossed(2)
    mine = row_of == me
    target_there = pick(mine, crossed(0))
    row_there = pick(mine, crossed(1))
    own_target, own_row, own_live = [pick(diagonal, table(0, which)) for which in range(3)]
    own_live_in = pick(mine, live_in)

    local = row_of.astype(F32)
    every = iota((peers * rows, lanes), 0)
    peer_of = sum(jnp.where(every // rows == s, peer[s], 0) for s in range(peers))
    same = peer_of == iota((peers * rows, lanes), 1) // slots
    every_local = (every % rows).astype(F32)

    back = jnp.where(local == own_row, own_live, 0.0).astype(BF16)
    there = jnp.where(same & (every_local == target_there), 1.0, 0.0).astype(BF16)
    back_table = lax.dot_general(back, there, NT, preferred_element_type=F32)
    into = jnp.where(local == own_target, own_live_in, 0.0)
    origin = jnp.where(same & (every_local == row_there), 1.0, 0.0).astype(BF16)
    table_ref[...] = lax.dot_general(into.astype(BF16), origin, NT, preferred_element_type=F32).astype(BF16)
    degree_ref[...] = jnp.broadcast_to(jnp.sum(into, axis=1, keepdims=True), degree_ref.shape)

    back_table = back_table + (iota(back_table.shape, 1) == iota(back_table.shape, 0)).astype(F32)
    degrees = []
    for s in range(peers):
        hit = jnp.where(local == pick(diagonal, table(s, 0)), pick(row_of == peer[s], live_in), 0.0)
        degrees.append(jnp.sum(hit, axis=1, keepdims=True))
    grad_mean = grads / (1.0 + jnp.concatenate(degrees, axis=0))
    high = grad_mean.astype(BF16)
    low = (grad_mean - high.astype(F32)).astype(BF16)
    back_table = back_table.astype(BF16)
    grad_hidden = self_ref[...] + jnp.dot(back_table, high, preferred_element_type=F32)
    grad_hidden = grad_hidden + jnp.dot(back_table, low, preferred_element_type=F32)
    grad_ref[...] = grad_hidden.astype(BF16)


def backward(near, far, w2s, w2n, peers, slots, rows_dev):
    width = w2s.shape[0]
    grad_self, near_grad, w2s, w2n = backward_near(near, w2s, w2n, rows_dev)
    grad, table, degree = pl.pallas_call(
        functools.partial(backward_kernel, peers, slots),
        in_specs=[VMEM] * 5,
        out_specs=[VMEM] * 3,
        out_shape=[
            jax.ShapeDtypeStruct((rows_dev, width), BF16),
            jax.ShapeDtypeStruct((rows_dev, peers * rows_dev), BF16),
            jax.ShapeDtypeStruct((rows_dev, 128), F32),
        ],
        name="second_backward", compiler_params=PARAMS,
        cost_estimate=pl.CostEstimate(flops=BACKWARD_COST, bytes_accessed=0, transcendentals=0),
    )(near, far, grad_self, near_grad, w2n)
    return grad, table, degree, w2s, w2n


def hidden_kernel(preact_ref, grad_ref, hidden_ref, grads_ref):
    preact = preact_ref[...]
    hidden_ref[...] = jnp.maximum(preact, 0.0).astype(BF16)
    grads_ref[0] = jnp.where(preact > 0, grad_ref[...], jnp.zeros_like(grad_ref))


def hidden_and_grads(preact, grad):
    return call(hidden_kernel, "hidden", (preact, grad), [(grad.shape, BF16), ((1,) + grad.shape, BF16)])


def own_part_kernel(hidden_ref, w2s_ref, out_ref):
    out_ref[...] = jnp.dot(hidden_ref[...], w2s_ref[...], preferred_element_type=F32)


def own_part(hidden, w2s):
    out = ((hidden.shape[0], w2s.shape[1]), F32)
    return call(own_part_kernel, "own_part", (hidden, w2s), [out], OWN_COST)[0]


def neigh_sum_kernel(near_ref, far_ref, table_ref, degree_ref, out_ref):
    rows, count = table_ref.shape[0], near_ref.shape[0]
    neigh_sum = jnp.dot(table_ref[:, :count], near_ref[...], preferred_element_type=F32)
    neigh_sum = neigh_sum + jnp.dot(table_ref[:, count:], far_ref[...], preferred_element_type=F32)
    out_ref[...] = ((near_ref[0:rows, :].astype(F32) + neigh_sum) / (1.0 + degree_ref[:, 0:1])).astype(BF16)


def mean_two(near, far, table, degree):
    out = ((table.shape[0], near.shape[1]), BF16)
    return call(neigh_sum_kernel, "mean_two", (near, far, table, degree), [out], MEAN_COST)[0]


def outputs_kernel(codes, mean_two_ref, own_ref, w2n_ref, *refs):
    grad_refs, (both_ref, out_hbm, self_hbm, neigh_hbm) = refs[:-9], refs[-9:-5]
    out_ref, self_ref, neigh_ref, grad_scratch, sems = refs[-5:]
    depth = both_ref.shape[0] // 2
    half = depth // 2 if depth % 32 == 0 else depth
    pieces = [(ref, hbm, n, at) for n, (ref, hbm) in enumerate(((self_ref, self_hbm), (neigh_ref, neigh_hbm)))
              for at in range(0, depth, half)]
    pairs = [(ref.at[0, pl.ds(at, half)], hbm.at[0, pl.ds(at, half)]) for ref, hbm, _, at in pieces]
    pairs.append((out_ref, out_hbm))
    copies = [pltpu.make_async_copy(src, dst, sems.at[n]) for n, (src, dst) in enumerate(pairs)]
    rows = mean_two_ref.shape[0]
    me = lax.axis_index("feat")
    for ref, code_list in zip(grad_refs, codes):
        for n, code in enumerate(code_list):
            to = pl.multiple_of(lax.bitwise_xor(me, code) * rows, rows)
            grad_scratch[pl.ds(to, rows), :] = ref[n]
    grad_pre = grad_scratch[...]
    for (ref, _, n, at), copy in zip(pieces, copies):
        columns = both_ref[n * depth + at : n * depth + at + half, :]
        ref[0, at : at + half] = jnp.dot(columns, grad_pre, preferred_element_type=F32)
        copy.start()

    out = own_ref[...] + jnp.dot(mean_two_ref[...], w2n_ref[...], preferred_element_type=F32)
    out_ref[0, 0] = out.astype(BF16)
    copies[-1].start()
    for copy in copies:
        copy.wait()


def outputs(mean, own, w2n, grads, codes, both):
    group, width = both.shape[1], grads[0].shape[2]
    grad = jax.ShapeDtypeStruct((1, both.shape[0] // 2, width), F32)
    out = jax.ShapeDtypeStruct((1, 1) + own.shape, BF16)
    return pl.pallas_call(
        functools.partial(outputs_kernel, codes),
        in_specs=[VMEM] * (len(grads) + 4),
        out_specs=[pl.BlockSpec(memory_space=pltpu.HBM)] * 3,
        out_shape=[out, grad, grad],
        scratch_shapes=[pltpu.VMEM(a.shape, a.dtype) for a in (out, grad, grad)]
        + [pltpu.VMEM((group, width), BF16), pltpu.SemaphoreType.DMA((5,))],
        name="outputs", compiler_params=PARAMS,
    )(mean, own, w2n, *grads, both)


def swap_cores(x):
    return lax.ppermute(x, "feat", [(i, i ^ 1) for i in range(lax.axis_size("feat"))])


def swap_chips(x, bits):
    return lax.ppermute(x, "feat", [(i, i ^ (2 * bits + 1)) for i in range(lax.axis_size("feat"))])


def swap_peers(x, level):
    feats, peers = lax.axis_size("feat"), lax.axis_size("dp")
    bits = 1 << level, 1 << (levels_of(peers) - 1 - level)
    pairs = [(f * peers + d, f * peers + (d ^ bits[f % 2])) for f in range(feats) for d in range(peers)]
    return lax.ppermute(x, ("feat", "dp"), pairs)


def gather_peers(x, cost, after):
    levels = levels_of(lax.axis_size("dp"))
    for level in range(levels - 1):
        x = join(x, swap_peers(x, level), cost, after)
    return x, swap_peers(x, levels - 1)


def on_device(features, neigh_lists, w1_self, w1_neigh, w2_self, w2_neigh, send_rows, send_count, recv_target, out_grad):
    chips, peers = lax.axis_size("feat") // 2, lax.axis_size("dp")
    rows_dev, slots = out_grad.shape[2], send_rows.shape[3]
    keep, send, both, aux = first_layer(
        features, neigh_lists, w1_self, w1_neigh, send_rows, send_count, recv_target, out_grad
    )
    parts = list(pair_sum(keep, swap_cores(send)))
    order = [chips // 2] + [s for s in range(chips - 1, 0, -1) if s != chips // 2]
    far = [swap_chips(parts[s], s) for s in order]
    aux_near, aux_far = gather_peers(aux, INDEX_COST, parts[:1])
    grad, table, degree, w2_self, w2_neigh = backward(
        aux_near, aux_far, w2_self, w2_neigh, peers, slots, rows_dev
    )
    hidden, grads = hidden_and_grads(preact_sum(parts[:1] + far), grad)
    codes, bits = [0], chips // 2
    while bits > 1:
        grads = join(grads, swap_chips(grads, bits))
        codes, bits = codes + [code ^ (2 * bits + 1) for code in codes], bits // 2
    near, far = gather_peers(hidden, HIDDEN_COST, (grads,))
    grads = [grads, swap_chips(grads, 1)]
    grads = grads + [swap_cores(x) for x in grads]
    codes = [[code ^ flip for code in codes] for flip in (0, 3, 1, 2)]
    mean = mean_two(near, far, table, degree)
    return outputs(mean, own_part(hidden, w2_self), w2_neigh, grads, codes, both)


def solution(mesh):
    in_specs = (
        P("dp", "feat", None),
        P("dp", None, None),
        P("feat", None),
        P("feat", None),
        P(),
        P(),
        P("dp", "feat", None, None),
        P("dp", "feat", None),
        P("dp", "feat", None, None),
        P("dp", "feat", None, None),
    )
    out_specs = (P("dp", "feat", None, None), P("dp", "feat", None), P("dp", "feat", None))
    return jax.shard_map(
        on_device, mesh=mesh, in_specs=in_specs, out_specs=out_specs, check_vma=False
    )
```

```python
import functools

import jax
import jax.numpy as jnp
from jax import lax
from jax.experimental import pallas as pl
from jax.experimental.pallas import tpu as pltpu
from jax.sharding import PartitionSpec as P

K1 = 10
HIDDEN_COST = 3 * 10**8
PREACT_COST = 4 * 10**8
OWN_COST = 10**8
BACKWARD_COST = 0
INDEX_COST = 10**9
F32 = jnp.float32
BF16 = jnp.bfloat16
NT = (((1,), (1,)), ((), ()))
TN = (((0,), (0,)), ((), ()))
VMEM = pl.BlockSpec(memory_space=pltpu.VMEM)
PARAMS = pltpu.CompilerParams(vmem_limit_bytes=12 * 1024 * 1024)


def iota(shape, dim):
    return lax.broadcasted_iota(jnp.int32, shape, dim)


def table_lanes(peers, slots):
    return -(-3 * peers * slots // 128) * 128


def first_layer_kernel(
    tiles, feat_hbm, lists_hbm, w1s_hbm, w1n_hbm, rows_hbm, counts_hbm, targets_hbm, og_hbm,
    keep_ref, send_ref, both_ref, aux_ref,
    feat_ref, lists_ref, w1_ref, rows_ref, counts_ref, targets_ref, og_ref, part_ref, sems,
):
    i = pl.program_id(0) if tiles > 1 else 0
    depth = feat_ref.shape[1]
    pairs = (
        (lists_hbm, lists_ref), (feat_hbm, feat_ref),
        (w1s_hbm, w1_ref.at[0:depth]), (w1n_hbm, w1_ref.at[depth : 2 * depth]),
        (targets_hbm, targets_ref), (rows_hbm, rows_ref), (counts_hbm, counts_ref), (og_hbm, og_ref),
    )
    copies = [pltpu.make_async_copy(src, dst, sems.at[n]) for n, (src, dst) in enumerate(pairs)]

    def once(step):
        if tiles > 1:
            pl.when(i == 0)(step)
        else:
            step()

    def wait(first, last):
        @once
        def _():
            for copy in copies[first:last]:
                copy.wait()

    @once
    def _():
        for copy in copies:
            copy.start()

    me = lax.axis_index("feat")
    core = me % 2
    nodes = feat_ref.shape[2]
    tile, width = part_ref.shape
    rows_dev = og_ref.shape[2]
    step = min(nodes, 256)
    at_tile = pl.ds(pl.multiple_of(i * tile, tile), tile) if tiles > 1 else slice(0, tile)
    wait(0, 1)
    hits = []
    for start in range(0, nodes, step):
        ids = iota((step, tile), 0) + start
        times = jnp.zeros((step, tile), F32)
        for k in range(K1):
            times = times + (ids == lists_ref[k, :, at_tile]).astype(F32)
        hits.append(times.astype(BF16))

    @once
    def _():
        for copy in copies[4:8]:
            copy.wait()
        peers, slots = rows_ref.shape[2], rows_ref.shape[3]
        lanes = aux_ref.shape[1] - width
        which = iota((slots, lanes), 1) // (peers * slots)
        same_slot = iota((slots, lanes), 1) % slots == iota((slots, lanes), 0)

        def tiled(ref, n):
            spread = (same_slot & (which == n)).astype(BF16)
            return jnp.dot(ref[0, 0].astype(BF16), spread, preferred_element_type=F32)

        eye = iota((peers, peers), 0) == iota((peers, peers), 1)
        column = jnp.sum(jnp.where(eye, counts_ref[0], 0), axis=1, keepdims=True)
        lane = iota((peers, lanes), 1)
        live = (lane // (peers * slots) == 2) & (lane % slots < column)
        tables = tiled(targets_ref, 0) + tiled(rows_ref, 1) + live.astype(F32)
        if peers < rows_dev:
            tables = jnp.concatenate([tables, jnp.zeros((rows_dev - peers, lanes), F32)], axis=0)
        aux_ref[:, :width] = og_ref[0, 0]
        aux_ref[:, width:] = tables.astype(BF16)

    wait(1, 2)
    total = jnp.zeros((depth, tile), F32)
    for n, times in enumerate(hits):
        total = total + jnp.dot(
            feat_ref[0, :, n * step : (n + 1) * step], times, preferred_element_type=F32
        )
    both_ref[0:depth, :] = feat_ref[0, :, at_tile]
    both_ref[depth:, :] = (total / K1).astype(BF16)
    wait(2, 4)
    part_ref[...] = lax.dot_general(both_ref[...], w1_ref[...], TN, preferred_element_type=F32)
    for z in range(keep_ref.shape[0]):
        kept = jnp.where(i * keep_ref.shape[0] + z == me // 2, core, 1 - core)
        for ref, which in ((keep_ref, kept), (send_ref, 1 - kept)):
            at = pl.multiple_of((2 * z + which) * rows_dev, rows_dev)
            ref[z] = part_ref[pl.ds(at, rows_dev), :]


def first_layer(features, lists, w1s, w1n, rows, counts, targets, og):
    depth = features.shape[1]
    group, width = lists.shape[2], w1s.shape[1]
    lists = lists.reshape(lists.shape[1], 1, group)
    rows_dev = og.shape[2]
    tile = min(group, 128)
    chips = group // (2 * rows_dev)
    tile_chips = tile // (2 * rows_dev)
    aux = (rows_dev, width + table_lanes(*rows.shape[2:]))
    args = (features, lists, w1s, w1n, rows, counts, targets, og)
    args = tuple(pltpu.with_memory_space_constraint(a, pltpu.HBM) for a in args)
    half = jax.ShapeDtypeStruct((chips, rows_dev, width), F32)
    half_spec = pl.BlockSpec((tile_chips, rows_dev, width), lambda i: (i, 0, 0))
    whole = lambda shape: pl.BlockSpec(shape, lambda i: (0,) * len(shape))
    scratch = [features, lists, jax.ShapeDtypeStruct((2 * depth, width), BF16), rows, counts, targets, og]
    return pl.pallas_call(
        functools.partial(first_layer_kernel, group // tile),
        grid=(group // tile,),
        in_specs=[pl.BlockSpec(memory_space=pltpu.HBM)] * len(args),
        out_specs=[
            half_spec, half_spec,
            pl.BlockSpec((2 * depth, tile), lambda i: (0, i)),
            whole(aux),
        ],
        out_shape=[
            half, half,
            jax.ShapeDtypeStruct((2 * depth, group), BF16),
            jax.ShapeDtypeStruct(aux, BF16),
        ],
        scratch_shapes=[pltpu.VMEM(a.shape, a.dtype) for a in scratch]
        + [pltpu.VMEM((tile, width), F32)]
        + [pltpu.SemaphoreType.DMA((len(args),))],
        name="first_layer", compiler_params=PARAMS,
    )(*args)


def call(kernel, name, args, out_shape, cost=0):
    return pl.pallas_call(
        kernel,
        in_specs=[VMEM] * len(args),
        out_specs=[VMEM] * len(out_shape),
        out_shape=[jax.ShapeDtypeStruct(shape, dtype) for shape, dtype in out_shape],
        name=name, compiler_params=PARAMS,
        cost_estimate=pl.CostEstimate(flops=cost, bytes_accessed=0, transcendentals=0),
    )(*args)


def reverse(n, levels):
    return sum(((n >> k) & 1) << (levels - 1 - k) for k in range(levels))


def code_of(n, levels, core):
    return jnp.where(core == 1, n, reverse(n, levels))


def levels_of(count):
    return count.bit_length() - 1


def pair_sum_kernel(keep_ref, got_ref, *outs):
    z = lax.axis_index("feat") // 2
    for s, ref in enumerate(outs):
        at = lax.bitwise_xor(z, s)
        ref[...] = keep_ref[at] + got_ref[at]


def pair_sum(keep, got):
    return call(pair_sum_kernel, "pair_sum", (keep, got), [(keep.shape[1:], F32)] * keep.shape[0])


def preact_kernel(*refs):
    refs[-1][...] = sum(ref[...] for ref in refs[:-1])


def preact_sum(parts):
    return call(preact_kernel, "preact", parts, [(parts[0].shape, F32)], PREACT_COST)[0]


def join_kernel(a_ref, b_ref, *refs):
    out_ref = refs[-1]
    count = a_ref.shape[0]
    out_ref[:count] = a_ref[...]
    out_ref[count:] = b_ref[...]


def join(a, b, cost=0, after=()):
    return call(join_kernel, "join", (a, b, *after), [((2 * a.shape[0],) + a.shape[1:], a.dtype)], cost)[0]


def near_kernel(near_ref, w2s_hbm, w2n_hbm, self_ref, near_grad_ref, w2s_ref, w2n_ref, sems):
    pairs = ((w2s_hbm, w2s_ref), (w2n_hbm, w2n_ref))
    copies = [pltpu.make_async_copy(src, dst, sems.at[n]) for n, (src, dst) in enumerate(pairs)]
    for copy in copies:
        copy.start()
    rows, width = self_ref.shape
    copies[0].wait()
    self_ref[...] = lax.dot_general(near_ref[:rows, :width], w2s_ref[...], NT, preferred_element_type=F32)
    copies[1].wait()
    near_grad_ref[...] = lax.dot_general(near_ref[:, :width], w2n_ref[...], NT, preferred_element_type=F32)


def backward_near(near, w2s, w2n, rows_dev):
    width = w2s.shape[0]
    hbm = pl.BlockSpec(memory_space=pltpu.HBM)
    shapes = [((rows_dev, width), F32), ((near.shape[0], width), F32), (w2s.shape, BF16), (w2n.shape, BF16)]
    return pl.pallas_call(
        near_kernel,
        in_specs=[VMEM, hbm, hbm],
        out_specs=[VMEM] * 4,
        out_shape=[jax.ShapeDtypeStruct(shape, dtype) for shape, dtype in shapes],
        scratch_shapes=[pltpu.SemaphoreType.DMA((2,))],
        name="backward_near", compiler_params=PARAMS,
        cost_estimate=pl.CostEstimate(flops=0, bytes_accessed=0, transcendentals=0),
    )(near, *[pltpu.with_memory_space_constraint(w, pltpu.HBM) for w in (w2s, w2n)])


def backward_kernel(
    peers, slots, near_ref, far_ref, self_ref, near_grad_ref, w2n_ref, grad_ref, table_ref, degree_ref
):
    me, core = lax.axis_index("dp"), lax.axis_index("feat") % 2
    rows, width = self_ref.shape
    lanes = peers * slots
    far_grad = lax.dot_general(far_ref[:, :width], w2n_ref[...], NT, preferred_element_type=F32)
    grads = jnp.concatenate([near_grad_ref[...], far_grad], axis=0)
    peer = [lax.bitwise_xor(me, code_of(s, levels_of(peers), core)) for s in range(peers)]

    def table(s, which):
        ref, at = (near_ref, s) if s < peers // 2 else (far_ref, s - peers // 2)
        at_lanes = slice(width + which * lanes, width + (which + 1) * lanes)
        return ref[at * rows : (at + 1) * rows, at_lanes].astype(F32)

    block_of = iota((rows, lanes), 1) // slots
    row_of = iota((rows, lanes), 0)
    diagonal = row_of == block_of

    def pick(where, x):
        return jnp.sum(jnp.where(where, x, 0.0), axis=0, keepdims=True)

    def crossed(which):
        return sum(jnp.where(block_of == peer[s], table(s, which), 0.0) for s in range(peers))

    live_in = crossed(2)
    mine = row_of == me
    target_there = pick(mine, crossed(0))
    row_there = pick(mine, crossed(1))
    own_target, own_row, own_live = [pick(diagonal, table(0, which)) for which in range(3)]
    own_live_in = pick(mine, live_in)

    local = row_of.astype(F32)
    every = iota((peers * rows, lanes), 0)
    peer_of = sum(jnp.where(every // rows == s, peer[s], 0) for s in range(peers))
    same = peer_of == iota((peers * rows, lanes), 1) // slots
    every_local = (every % rows).astype(F32)

    back = jnp.where(local == own_row, own_live, 0.0).astype(BF16)
    there = jnp.where(same & (every_local == target_there), 1.0, 0.0).astype(BF16)
    back_table = lax.dot_general(back, there, NT, preferred_element_type=F32)
    into = jnp.where(local == own_target, own_live_in, 0.0)
    origin = jnp.where(same & (every_local == row_there), 1.0, 0.0).astype(BF16)
    table_ref[...] = lax.dot_general(into.astype(BF16), origin, NT, preferred_element_type=F32).astype(BF16)
    degree_ref[...] = jnp.broadcast_to(jnp.sum(into, axis=1, keepdims=True), degree_ref.shape)

    back_table = back_table + (iota(back_table.shape, 1) == iota(back_table.shape, 0)).astype(F32)
    degrees = []
    for s in range(peers):
        hit = jnp.where(local == pick(diagonal, table(s, 0)), pick(row_of == peer[s], live_in), 0.0)
        degrees.append(jnp.sum(hit, axis=1, keepdims=True))
    grad_mean = grads / (1.0 + jnp.concatenate(degrees, axis=0))
    high = grad_mean.astype(BF16)
    low = (grad_mean - high.astype(F32)).astype(BF16)
    back_table = back_table.astype(BF16)
    grad_hidden = self_ref[...] + jnp.dot(back_table, high, preferred_element_type=F32)
    grad_hidden = grad_hidden + jnp.dot(back_table, low, preferred_element_type=F32)
    grad_ref[...] = grad_hidden.astype(BF16)


def backward(near, far, w2s, w2n, peers, slots, rows_dev):
    width = w2s.shape[0]
    grad_self, near_grad, w2s, w2n = backward_near(near, w2s, w2n, rows_dev)
    grad, table, degree = pl.pallas_call(
        functools.partial(backward_kernel, peers, slots),
        in_specs=[VMEM] * 5,
        out_specs=[VMEM] * 3,
        out_shape=[
            jax.ShapeDtypeStruct((rows_dev, width), BF16),
            jax.ShapeDtypeStruct((rows_dev, peers * rows_dev), BF16),
            jax.ShapeDtypeStruct((rows_dev, 128), F32),
        ],
        name="second_backward", compiler_params=PARAMS,
        cost_estimate=pl.CostEstimate(flops=BACKWARD_COST, bytes_accessed=0, transcendentals=0),
    )(near, far, grad_self, near_grad, w2n)
    return grad, table, degree, w2s, w2n


def hidden_kernel(preact_ref, grad_ref, hidden_ref, grads_ref):
    preact = preact_ref[...]
    hidden_ref[...] = jnp.maximum(preact, 0.0).astype(BF16)
    grads_ref[0] = jnp.where(preact > 0, grad_ref[...], jnp.zeros_like(grad_ref))


def hidden_and_grads(preact, grad):
    return call(hidden_kernel, "hidden", (preact, grad), [(grad.shape, BF16), ((1,) + grad.shape, BF16)])


def own_part_kernel(hidden_ref, w2s_ref, out_ref):
    out_ref[...] = jnp.dot(hidden_ref[...], w2s_ref[...], preferred_element_type=F32)


def own_part(hidden, w2s):
    out = ((hidden.shape[0], w2s.shape[1]), F32)
    return call(own_part_kernel, "own_part", (hidden, w2s), [out], OWN_COST)[0]


def outputs_kernel(codes, near_ref, far_ref, table_ref, degree_ref, own_ref, w2n_ref, *refs):
    grad_refs, (both_ref, out_hbm, self_hbm, neigh_hbm) = refs[:-9], refs[-9:-5]
    out_ref, self_ref, neigh_ref, grad_scratch, sems = refs[-5:]
    depth = both_ref.shape[0] // 2
    half = depth // 2 if depth % 32 == 0 else depth
    pieces = [(ref, hbm, n, at) for n, (ref, hbm) in enumerate(((self_ref, self_hbm), (neigh_ref, neigh_hbm)))
              for at in range(0, depth, half)]
    pairs = [(ref.at[0, pl.ds(at, half)], hbm.at[0, pl.ds(at, half)]) for ref, hbm, _, at in pieces]
    pairs.append((out_ref, out_hbm))
    copies = [pltpu.make_async_copy(src, dst, sems.at[n]) for n, (src, dst) in enumerate(pairs)]
    rows = table_ref.shape[0]
    me = lax.axis_index("feat")
    for ref, code_list in zip(grad_refs, codes):
        for n, code in enumerate(code_list):
            to = pl.multiple_of(lax.bitwise_xor(me, code) * rows, rows)
            grad_scratch[pl.ds(to, rows), :] = ref[n]
    grad_pre = grad_scratch[...]
    for (ref, _, n, at), copy in zip(pieces, copies):
        columns = both_ref[n * depth + at : n * depth + at + half, :]
        ref[0, at : at + half] = jnp.dot(columns, grad_pre, preferred_element_type=F32)
        copy.start()

    count = near_ref.shape[0]
    neigh_sum = jnp.dot(table_ref[:, :count], near_ref[...], preferred_element_type=F32)
    neigh_sum = neigh_sum + jnp.dot(table_ref[:, count:], far_ref[...], preferred_element_type=F32)
    mean_two = ((near_ref[0:rows, :].astype(F32) + neigh_sum) / (1.0 + degree_ref[:, 0:1])).astype(BF16)
    out = own_ref[...] + jnp.dot(mean_two, w2n_ref[...], preferred_element_type=F32)
    out_ref[0, 0] = out.astype(BF16)
    copies[-1].start()
    for copy in copies:
        copy.wait()


def outputs(near, far, table, degree, own, w2n, grads, codes, both):
    group, width = both.shape[1], grads[0].shape[2]
    grad = jax.ShapeDtypeStruct((1, both.shape[0] // 2, width), F32)
    out = jax.ShapeDtypeStruct((1, 1) + own.shape, BF16)
    return pl.pallas_call(
        functools.partial(outputs_kernel, codes),
        in_specs=[VMEM] * (len(grads) + 7),
        out_specs=[pl.BlockSpec(memory_space=pltpu.HBM)] * 3,
        out_shape=[out, grad, grad],
        scratch_shapes=[pltpu.VMEM(a.shape, a.dtype) for a in (out, grad, grad)]
        + [pltpu.VMEM((group, width), BF16), pltpu.SemaphoreType.DMA((5,))],
        name="outputs", compiler_params=PARAMS,
    )(near, far, table, degree, own, w2n, *grads, both)


def swap_cores(x):
    return lax.ppermute(x, "feat", [(i, i ^ 1) for i in range(lax.axis_size("feat"))])


def swap_chips(x, bits):
    return lax.ppermute(x, "feat", [(i, i ^ (2 * bits + 1)) for i in range(lax.axis_size("feat"))])


def swap_peers(x, level):
    feats, peers = lax.axis_size("feat"), lax.axis_size("dp")
    bits = 1 << (levels_of(peers) - 1 - level), 1 << level
    pairs = [(f * peers + d, f * peers + (d ^ bits[f % 2])) for f in range(feats) for d in range(peers)]
    return lax.ppermute(x, ("feat", "dp"), pairs)


def gather_peers(x, cost, after):
    levels = levels_of(lax.axis_size("dp"))
    for level in range(levels - 1):
        x = join(x, swap_peers(x, level), cost, after)
    return x, swap_peers(x, levels - 1)


def on_device(features, neigh_lists, w1_self, w1_neigh, w2_self, w2_neigh, send_rows, send_count, recv_target, out_grad):
    chips, peers = lax.axis_size("feat") // 2, lax.axis_size("dp")
    rows_dev, slots = out_grad.shape[2], send_rows.shape[3]
    keep, send, both, aux = first_layer(
        features, neigh_lists, w1_self, w1_neigh, send_rows, send_count, recv_target, out_grad
    )
    parts = list(pair_sum(keep, swap_cores(send)))
    order = [chips // 2] + [s for s in range(chips - 1, 0, -1) if s != chips // 2]
    far = [swap_chips(parts[s], s) for s in order]
    aux_near, aux_far = gather_peers(aux, INDEX_COST, parts[:1])
    grad, table, degree, w2_self, w2_neigh = backward(
        aux_near, aux_far, w2_self, w2_neigh, peers, slots, rows_dev
    )
    hidden, grads = hidden_and_grads(preact_sum(parts[:1] + far), grad)
    pieces, codes, bits = [grads], [[0]], chips // 2
    while bits:
        pieces.append(swap_chips(grads, bits))
        codes.append([code ^ (2 * bits + 1) for known in codes for code in known])
        bits //= 2
        if bits:
            grads = join(grads, pieces[-1])
    near, far = gather_peers(hidden, HIDDEN_COST, (grads,))
    pieces = pieces + [swap_cores(x) for x in pieces]
    codes = codes + [[code ^ 1 for code in known] for known in codes]
    own = own_part(hidden, w2_self)
    return outputs(near, far, table, degree, own, w2_neigh, pieces, codes, both)


def solution(mesh):
    in_specs = (
        P("dp", "feat", None),
        P("dp", None, None),
        P("feat", None),
        P("feat", None),
        P(),
        P(),
        P("dp", "feat", None, None),
        P("dp", "feat", None),
        P("dp", "feat", None, None),
        P("dp", "feat", None, None),
    )
    out_specs = (P("dp", "feat", None, None), P("dp", "feat", None), P("dp", "feat", None))
    return jax.shard_map(
        on_device, mesh=mesh, in_specs=in_specs, out_specs=out_specs, check_vma=False
    )
```

```python
import functools

import jax
import jax.numpy as jnp
from jax import lax
from jax.experimental import pallas as pl
from jax.experimental.pallas import tpu as pltpu
from jax.sharding import PartitionSpec as P

K1 = 10
HIDDEN_COST = 3 * 10**8
PREACT_COST = 4 * 10**8
OWN_COST = 10**8
BACKWARD_COST = 0
INDEX_COST = 10**9
F32 = jnp.float32
BF16 = jnp.bfloat16
NT = (((1,), (1,)), ((), ()))
TN = (((0,), (0,)), ((), ()))
VMEM = pl.BlockSpec(memory_space=pltpu.VMEM)
PARAMS = pltpu.CompilerParams(vmem_limit_bytes=12 * 1024 * 1024)


def iota(shape, dim):
    return lax.broadcasted_iota(jnp.int32, shape, dim)


def table_lanes(peers, slots):
    return -(-3 * peers * slots // 128) * 128


def first_layer_kernel(
    tiles, feat_hbm, lists_hbm, w1s_hbm, w1n_hbm, rows_hbm, counts_hbm, targets_hbm, og_hbm,
    keep_ref, send_ref, both_ref, aux_ref,
    feat_ref, lists_ref, w1_ref, rows_ref, counts_ref, targets_ref, og_ref, part_ref, sems,
):
    i = pl.program_id(0) if tiles > 1 else 0
    depth = feat_ref.shape[1]
    pairs = (
        (lists_hbm, lists_ref), (feat_hbm, feat_ref),
        (w1s_hbm, w1_ref.at[0:depth]), (w1n_hbm, w1_ref.at[depth : 2 * depth]),
        (targets_hbm, targets_ref), (rows_hbm, rows_ref), (counts_hbm, counts_ref), (og_hbm, og_ref),
    )
    copies = [pltpu.make_async_copy(src, dst, sems.at[n]) for n, (src, dst) in enumerate(pairs)]

    def once(step):
        if tiles > 1:
            pl.when(i == 0)(step)
        else:
            step()

    def wait(first, last):
        @once
        def _():
            for copy in copies[first:last]:
                copy.wait()

    @once
    def _():
        for copy in copies:
            copy.start()

    me = lax.axis_index("feat")
    core = me % 2
    nodes = feat_ref.shape[2]
    tile, width = part_ref.shape
    rows_dev = og_ref.shape[2]
    step = min(nodes, 256)
    at_tile = pl.ds(pl.multiple_of(i * tile, tile), tile) if tiles > 1 else slice(0, tile)
    wait(0, 1)
    hits = []
    for start in range(0, nodes, step):
        ids = iota((step, tile), 0) + start
        times = jnp.zeros((step, tile), F32)
        for k in range(K1):
            times = times + (ids == lists_ref[k, :, at_tile]).astype(F32)
        hits.append(times.astype(BF16))

    @once
    def _():
        for copy in copies[4:8]:
            copy.wait()
        peers, slots = rows_ref.shape[2], rows_ref.shape[3]
        lanes = aux_ref.shape[1] - width
        which = iota((slots, lanes), 1) // (peers * slots)
        same_slot = iota((slots, lanes), 1) % slots == iota((slots, lanes), 0)

        def tiled(ref, n):
            spread = (same_slot & (which == n)).astype(BF16)
            return jnp.dot(ref[0, 0].astype(BF16), spread, preferred_element_type=F32)

        eye = iota((peers, peers), 0) == iota((peers, peers), 1)
        column = jnp.sum(jnp.where(eye, counts_ref[0], 0), axis=1, keepdims=True)
        lane = iota((peers, lanes), 1)
        live = (lane // (peers * slots) == 2) & (lane % slots < column)
        tables = tiled(targets_ref, 0) + tiled(rows_ref, 1) + live.astype(F32)
        if peers < rows_dev:
            tables = jnp.concatenate([tables, jnp.zeros((rows_dev - peers, lanes), F32)], axis=0)
        aux_ref[:, :width] = og_ref[0, 0]
        aux_ref[:, width:] = tables.astype(BF16)

    wait(1, 2)
    total = jnp.zeros((depth, tile), F32)
    for n, times in enumerate(hits):
        total = total + jnp.dot(
            feat_ref[0, :, n * step : (n + 1) * step], times, preferred_element_type=F32
        )
    both_ref[0:depth, :] = feat_ref[0, :, at_tile]
    both_ref[depth:, :] = (total / K1).astype(BF16)
    wait(2, 4)
    part_ref[...] = lax.dot_general(both_ref[...], w1_ref[...], TN, preferred_element_type=F32)
    for z in range(keep_ref.shape[0]):
        kept = jnp.where(i * keep_ref.shape[0] + z == me // 2, core, 1 - core)
        for ref, which in ((keep_ref, kept), (send_ref, 1 - kept)):
            at = pl.multiple_of((2 * z + which) * rows_dev, rows_dev)
            ref[z] = part_ref[pl.ds(at, rows_dev), :]


def first_layer(features, lists, w1s, w1n, rows, counts, targets, og):
    depth = features.shape[1]
    group, width = lists.shape[2], w1s.shape[1]
    lists = lists.reshape(lists.shape[1], 1, group)
    rows_dev = og.shape[2]
    tile = min(group, 128)
    chips = group // (2 * rows_dev)
    tile_chips = tile // (2 * rows_dev)
    aux = (rows_dev, width + table_lanes(*rows.shape[2:]))
    args = (features, lists, w1s, w1n, rows, counts, targets, og)
    args = tuple(pltpu.with_memory_space_constraint(a, pltpu.HBM) for a in args)
    half = jax.ShapeDtypeStruct((chips, rows_dev, width), F32)
    half_spec = pl.BlockSpec((tile_chips, rows_dev, width), lambda i: (i, 0, 0))
    whole = lambda shape: pl.BlockSpec(shape, lambda i: (0,) * len(shape))
    scratch = [features, lists, jax.ShapeDtypeStruct((2 * depth, width), BF16), rows, counts, targets, og]
    return pl.pallas_call(
        functools.partial(first_layer_kernel, group // tile),
        grid=(group // tile,),
        in_specs=[pl.BlockSpec(memory_space=pltpu.HBM)] * len(args),
        out_specs=[
            half_spec, half_spec,
            pl.BlockSpec((2 * depth, tile), lambda i: (0, i)),
            whole(aux),
        ],
        out_shape=[
            half, half,
            jax.ShapeDtypeStruct((2 * depth, group), BF16),
            jax.ShapeDtypeStruct(aux, BF16),
        ],
        scratch_shapes=[pltpu.VMEM(a.shape, a.dtype) for a in scratch]
        + [pltpu.VMEM((tile, width), F32)]
        + [pltpu.SemaphoreType.DMA((len(args),))],
        name="first_layer", compiler_params=PARAMS,
    )(*args)


def call(kernel, name, args, out_shape, cost=0):
    return pl.pallas_call(
        kernel,
        in_specs=[VMEM] * len(args),
        out_specs=[VMEM] * len(out_shape),
        out_shape=[jax.ShapeDtypeStruct(shape, dtype) for shape, dtype in out_shape],
        name=name, compiler_params=PARAMS,
        cost_estimate=pl.CostEstimate(flops=cost, bytes_accessed=0, transcendentals=0),
    )(*args)


def reverse(n, levels):
    return sum(((n >> k) & 1) << (levels - 1 - k) for k in range(levels))


def code_of(n, levels, core):
    return jnp.where(core == 0, n, reverse(n, levels))


def levels_of(count):
    return count.bit_length() - 1


def pair_sum_kernel(keep_ref, got_ref, *outs):
    z = lax.axis_index("feat") // 2
    for s, ref in enumerate(outs):
        at = lax.bitwise_xor(z, s)
        ref[...] = keep_ref[at] + got_ref[at]


def pair_sum(keep, got):
    return call(pair_sum_kernel, "pair_sum", (keep, got), [(keep.shape[1:], F32)] * keep.shape[0])


def preact_kernel(*refs):
    refs[-1][...] = sum(ref[...] for ref in refs[:-1])


def preact_sum(parts):
    return call(preact_kernel, "preact", parts, [(parts[0].shape, F32)], PREACT_COST)[0]


def join_kernel(a_ref, b_ref, *refs):
    out_ref = refs[-1]
    count = a_ref.shape[0]
    out_ref[:count] = a_ref[...]
    out_ref[count:] = b_ref[...]


def join(a, b, cost=0, after=()):
    return call(join_kernel, "join", (a, b, *after), [((2 * a.shape[0],) + a.shape[1:], a.dtype)], cost)[0]


def near_kernel(near_ref, w2s_hbm, w2n_hbm, self_ref, near_grad_ref, w2s_ref, w2n_ref, sems):
    pairs = ((w2s_hbm, w2s_ref), (w2n_hbm, w2n_ref))
    copies = [pltpu.make_async_copy(src, dst, sems.at[n]) for n, (src, dst) in enumerate(pairs)]
    for copy in copies:
        copy.start()
    rows, width = self_ref.shape
    copies[0].wait()
    self_ref[...] = lax.dot_general(near_ref[:rows, :width], w2s_ref[...], NT, preferred_element_type=F32)
    copies[1].wait()
    near_grad_ref[...] = lax.dot_general(near_ref[:, :width], w2n_ref[...], NT, preferred_element_type=F32)


def backward_near(near, w2s, w2n, rows_dev):
    width = w2s.shape[0]
    hbm = pl.BlockSpec(memory_space=pltpu.HBM)
    shapes = [((rows_dev, width), F32), ((near.shape[0], width), F32), (w2s.shape, BF16), (w2n.shape, BF16)]
    return pl.pallas_call(
        near_kernel,
        in_specs=[VMEM, hbm, hbm],
        out_specs=[VMEM] * 4,
        out_shape=[jax.ShapeDtypeStruct(shape, dtype) for shape, dtype in shapes],
        scratch_shapes=[pltpu.SemaphoreType.DMA((2,))],
        name="backward_near", compiler_params=PARAMS,
        cost_estimate=pl.CostEstimate(flops=0, bytes_accessed=0, transcendentals=0),
    )(near, *[pltpu.with_memory_space_constraint(w, pltpu.HBM) for w in (w2s, w2n)])


def backward_kernel(
    peers, slots, near_ref, far_ref, self_ref, near_grad_ref, w2n_ref, grad_ref, table_ref, degree_ref
):
    me, core = lax.axis_index("dp"), lax.axis_index("feat") % 2
    rows, width = self_ref.shape
    lanes = peers * slots
    far_grad = lax.dot_general(far_ref[:, :width], w2n_ref[...], NT, preferred_element_type=F32)
    grads = jnp.concatenate([near_grad_ref[...], far_grad], axis=0)
    peer = [lax.bitwise_xor(me, code_of(s, levels_of(peers), core)) for s in range(peers)]

    def table(s, which):
        ref, at = (near_ref, s) if s < peers // 2 else (far_ref, s - peers // 2)
        at_lanes = slice(width + which * lanes, width + (which + 1) * lanes)
        return ref[at * rows : (at + 1) * rows, at_lanes].astype(F32)

    block_of = iota((rows, lanes), 1) // slots
    row_of = iota((rows, lanes), 0)
    diagonal = row_of == block_of

    def pick(where, x):
        return jnp.sum(jnp.where(where, x, 0.0), axis=0, keepdims=True)

    def crossed(which):
        return sum(jnp.where(block_of == peer[s], table(s, which), 0.0) for s in range(peers))

    live_in = crossed(2)
    mine = row_of == me
    target_there = pick(mine, crossed(0))
    row_there = pick(mine, crossed(1))
    own_target, own_row, own_live = [pick(diagonal, table(0, which)) for which in range(3)]
    own_live_in = pick(mine, live_in)

    local = row_of.astype(F32)
    every = iota((peers * rows, lanes), 0)
    peer_of = sum(jnp.where(every // rows == s, peer[s], 0) for s in range(peers))
    same = peer_of == iota((peers * rows, lanes), 1) // slots
    every_local = (every % rows).astype(F32)

    back = jnp.where(local == own_row, own_live, 0.0).astype(BF16)
    there = jnp.where(same & (every_local == target_there), 1.0, 0.0).astype(BF16)
    back_table = lax.dot_general(back, there, NT, preferred_element_type=F32)
    into = jnp.where(local == own_target, own_live_in, 0.0)
    origin = jnp.where(same & (every_local == row_there), 1.0, 0.0).astype(BF16)
    table_ref[...] = lax.dot_general(into.astype(BF16), origin, NT, preferred_element_type=F32).astype(BF16)
    degree_ref[...] = jnp.broadcast_to(jnp.sum(into, axis=1, keepdims=True), degree_ref.shape)

    back_table = back_table + (iota(back_table.shape, 1) == iota(back_table.shape, 0)).astype(F32)
    degrees = []
    for s in range(peers):
        hit = jnp.where(local == pick(diagonal, table(s, 0)), pick(row_of == peer[s], live_in), 0.0)
        degrees.append(jnp.sum(hit, axis=1, keepdims=True))
    grad_mean = grads / (1.0 + jnp.concatenate(degrees, axis=0))
    high = grad_mean.astype(BF16)
    low = (grad_mean - high.astype(F32)).astype(BF16)
    back_table = back_table.astype(BF16)
    grad_hidden = self_ref[...] + jnp.dot(back_table, high, preferred_element_type=F32)
    grad_hidden = grad_hidden + jnp.dot(back_table, low, preferred_element_type=F32)
    grad_ref[...] = grad_hidden.astype(BF16)


def backward(near, far, w2s, w2n, peers, slots, rows_dev):
    width = w2s.shape[0]
    grad_self, near_grad, w2s, w2n = backward_near(near, w2s, w2n, rows_dev)
    grad, table, degree = pl.pallas_call(
        functools.partial(backward_kernel, peers, slots),
        in_specs=[VMEM] * 5,
        out_specs=[VMEM] * 3,
        out_shape=[
            jax.ShapeDtypeStruct((rows_dev, width), BF16),
            jax.ShapeDtypeStruct((rows_dev, peers * rows_dev), BF16),
            jax.ShapeDtypeStruct((rows_dev, 128), F32),
        ],
        name="second_backward", compiler_params=PARAMS,
        cost_estimate=pl.CostEstimate(flops=BACKWARD_COST, bytes_accessed=0, transcendentals=0),
    )(near, far, grad_self, near_grad, w2n)
    return grad, table, degree, w2s, w2n


def hidden_kernel(preact_ref, grad_ref, hidden_ref, grads_ref):
    preact = preact_ref[...]
    hidden_ref[...] = jnp.maximum(preact, 0.0).astype(BF16)
    grads_ref[0] = jnp.where(preact > 0, grad_ref[...], jnp.zeros_like(grad_ref))


def hidden_and_grads(preact, grad):
    return call(hidden_kernel, "hidden", (preact, grad), [(grad.shape, BF16), ((1,) + grad.shape, BF16)])


def own_part_kernel(hidden_ref, w2s_ref, out_ref):
    out_ref[...] = jnp.dot(hidden_ref[...], w2s_ref[...], preferred_element_type=F32)


def own_part(hidden, w2s):
    out = ((hidden.shape[0], w2s.shape[1]), F32)
    return call(own_part_kernel, "own_part", (hidden, w2s), [out], OWN_COST)[0]


def outputs_kernel(codes, near_ref, far_ref, table_ref, degree_ref, own_ref, w2n_ref, *refs):
    grad_refs, (both_ref, out_hbm, self_hbm, neigh_hbm) = refs[:-9], refs[-9:-5]
    out_ref, self_ref, neigh_ref, grad_scratch, sems = refs[-5:]
    depth = both_ref.shape[0] // 2
    half = depth
    pieces = [(ref, hbm, n, at) for n, (ref, hbm) in enumerate(((self_ref, self_hbm), (neigh_ref, neigh_hbm)))
              for at in range(0, depth, half)]
    pairs = [(ref.at[0, pl.ds(at, half)], hbm.at[0, pl.ds(at, half)]) for ref, hbm, _, at in pieces]
    pairs.append((out_ref, out_hbm))
    copies = [pltpu.make_async_copy(src, dst, sems.at[n]) for n, (src, dst) in enumerate(pairs)]
    rows = table_ref.shape[0]
    me = lax.axis_index("feat")
    for ref, code_list in zip(grad_refs, codes):
        for n, code in enumerate(code_list):
            to = pl.multiple_of(lax.bitwise_xor(me, code) * rows, rows)
            grad_scratch[pl.ds(to, rows), :] = ref[n]
    count = near_ref.shape[0]
    neigh_sum = jnp.dot(table_ref[:, :count], near_ref[...], preferred_element_type=F32)
    neigh_sum = neigh_sum + jnp.dot(table_ref[:, count:], far_ref[...], preferred_element_type=F32)
    mean_two = ((near_ref[0:rows, :].astype(F32) + neigh_sum) / (1.0 + degree_ref[:, 0:1])).astype(BF16)
    out = own_ref[...] + jnp.dot(mean_two, w2n_ref[...], preferred_element_type=F32)
    out_ref[0, 0] = out.astype(BF16)
    copies[-1].start()
    grad_pre = grad_scratch[...]
    for (ref, _, n, at), copy in zip(pieces, copies):
        columns = both_ref[n * depth + at : n * depth + at + half, :]
        ref[0, at : at + half] = jnp.dot(columns, grad_pre, preferred_element_type=F32)
        copy.start()
    for copy in copies:
        copy.wait()


def outputs(near, far, table, degree, own, w2n, grads, codes, both):
    group, width = both.shape[1], grads[0].shape[2]
    grad = jax.ShapeDtypeStruct((1, both.shape[0] // 2, width), F32)
    out = jax.ShapeDtypeStruct((1, 1) + own.shape, BF16)
    return pl.pallas_call(
        functools.partial(outputs_kernel, codes),
        in_specs=[VMEM] * (len(grads) + 7),
        out_specs=[pl.BlockSpec(memory_space=pltpu.HBM)] * 3,
        out_shape=[out, grad, grad],
        scratch_shapes=[pltpu.VMEM(a.shape, a.dtype) for a in (out, grad, grad)]
        + [pltpu.VMEM((group, width), BF16), pltpu.SemaphoreType.DMA((5,))],
        name="outputs", compiler_params=PARAMS,
    )(near, far, table, degree, own, w2n, *grads, both)


def swap_cores(x):
    return lax.ppermute(x, "feat", [(i, i ^ 1) for i in range(lax.axis_size("feat"))])


def swap_chips(x, bits):
    return lax.ppermute(x, "feat", [(i, i ^ (2 * bits + 1)) for i in range(lax.axis_size("feat"))])


def swap_peers(x, level):
    feats, peers = lax.axis_size("feat"), lax.axis_size("dp")
    bits = 1 << level, 1 << (levels_of(peers) - 1 - level)
    pairs = [(f * peers + d, f * peers + (d ^ bits[f % 2])) for f in range(feats) for d in range(peers)]
    return lax.ppermute(x, ("feat", "dp"), pairs)


def gather_peers(x, cost, after):
    levels = levels_of(lax.axis_size("dp"))
    for level in range(levels - 1):
        x = join(x, swap_peers(x, level), cost, after)
    return x, swap_peers(x, levels - 1)


def on_device(features, neigh_lists, w1_self, w1_neigh, w2_self, w2_neigh, send_rows, send_count, recv_target, out_grad):
    chips, peers = lax.axis_size("feat") // 2, lax.axis_size("dp")
    rows_dev, slots = out_grad.shape[2], send_rows.shape[3]
    keep, send, both, aux = first_layer(
        features, neigh_lists, w1_self, w1_neigh, send_rows, send_count, recv_target, out_grad
    )
    parts = list(pair_sum(keep, swap_cores(send)))
    order = [chips // 2] + [s for s in range(chips - 1, 0, -1) if s != chips // 2]
    far = [swap_chips(parts[s], s) for s in order]
    aux_near, aux_far = gather_peers(aux, INDEX_COST, parts[:1])
    grad, table, degree, w2_self, w2_neigh = backward(
        aux_near, aux_far, w2_self, w2_neigh, peers, slots, rows_dev
    )
    hidden, grads = hidden_and_grads(preact_sum(parts[:1] + far), grad)
    pieces, codes, bits = [grads], [[0]], chips // 2
    while bits:
        pieces.append(swap_chips(grads, bits))
        codes.append([code ^ (2 * bits + 1) for known in codes for code in known])
        bits //= 2
        if bits:
            grads = join(grads, pieces[-1])
    near, far = gather_peers(hidden, HIDDEN_COST, (grads,))
    pieces = pieces + [swap_cores(x) for x in pieces]
    codes = codes + [[code ^ 1 for code in known] for known in codes]
    own = own_part(hidden, w2_self)
    return outputs(near, far, table, degree, own, w2_neigh, pieces, codes, both)


def solution(mesh):
    in_specs = (
        P("dp", "feat", None),
        P("dp", None, None),
        P("feat", None),
        P("feat", None),
        P(),
        P(),
        P("dp", "feat", None, None),
        P("dp", "feat", None),
        P("dp", "feat", None, None),
        P("dp", "feat", None, None),
    )
    out_specs = (P("dp", "feat", None, None), P("dp", "feat", None), P("dp", "feat", None))
    return jax.shard_map(
        on_device, mesh=mesh, in_specs=in_specs, out_specs=out_specs, check_vma=False
    )
```
